32 devices in a mesh: grp: 8 (over y, x, core), mem: 4 (over z).
Axes of the slice: x: 2, y: 2, z: 4, core: 2. Of those that a mesh axis runs over, the one named last changes fastest.
Arguments:
- stem: bfloat16 [2, 8, 4, 1024, 256], P(None, 'grp', 'mem'), may hold values from -6 to 6
- branches: bfloat16 [3, 2, 256, 256], replicated, may hold values from -0.25 to 0.25
- mode_order: int32 [3, 256], replicated, may hold values from 0 to 255, each once within a row
Outputs:
- contracted: bfloat16 [2, 8, 4, 1024, 256], P(None, 'grp', 'mem')
The draws below stay inside these ranges and needn't reach their ends.
Inputs may be any that keep to these rules, and one draw needn't show every extreme that they name: Each row of mode_order names every number below 256 once.
All inputs are finite; a program needn't handle non-finite values.
Results may differ from the reference program's by a relative error of at most 0.0057.
Values may be sent and summed in bfloat16 or wider, within the bound.
No kernel may reach another device: no remote copies, remote signals or barrier semaphores. Data moves between devices by JAX's collectives and lax.ppermute only.
A program may use at most 64 MiB of HBM per device.

```python
import jax
import jax.numpy as jnp
from jax import lax

BLOCK = 256
ROWS = 1024
NG = 8
NM = 4
U2 = 64
U3 = 32


def levels(own_key, shape, shards, low, high):
    level, own = 1.0, jax.random.fold_in(own_key, 6)
    for dim, shards_of in shards:
        steps = jnp.exp(jax.random.uniform(jax.random.fold_in(own, dim), (shards_of,), jnp.float32, low / len(shards), high / len(shards)))
        level = level * jnp.repeat(steps, shape[dim] // shards_of).reshape([-1 if axis == dim else 1 for axis in range(len(shape))])
    return level


def centred(own_key, shape, deviation, bound, split=(), dtype=jnp.bfloat16):
    array = deviation * jax.random.normal(own_key, shape, jnp.float32)
    if split:
        array = array * levels(own_key, shape, split, -0.22, 0.18)
    return jnp.clip(array, -bound, bound).astype(dtype)


def setup_inputs(seed: int = 0) -> dict:
    key_list = jax.random.split(jax.random.key(seed), 4)
    return {
        "stem": centred(key_list[0], (2, NG, NM, ROWS, BLOCK), 1.0, 6.0, ((1, 8), (2, 4))),
        "branches": centred(key_list[1], (3, 2, BLOCK, BLOCK), (2 * BLOCK) ** -0.5, 0.25),
        "mode_order": jax.vmap(lambda own: jax.random.permutation(own, BLOCK))(jax.random.split(key_list[2], 3)).reshape((3, BLOCK)).astype(jnp.int32),
    }


def real_matrix(branches, mode_order, section_no):
    weight = branches[section_no][:, mode_order[section_no], :]
    upper = jnp.concatenate([weight[0], weight[1]], axis=1)
    lower = jnp.concatenate([-weight[1], weight[0]], axis=1)
    return jnp.concatenate([upper, lower], axis=0)


def contract(stem_view, branches, mode_order, section_no):
    real_form = real_matrix(branches, mode_order, section_no)

    def one_slab(slab_data):
        joined = jnp.concatenate([slab_data[0], slab_data[1]], axis=-1)
        result = jnp.dot(joined, real_form, preferred_element_type=jnp.float32)
        return jnp.stack([result[..., :BLOCK], result[..., BLOCK:]]).astype(jnp.bfloat16)

    mapped = lax.map(one_slab, jnp.moveaxis(stem_view, 1, 0))
    return jnp.moveaxis(mapped, 0, 1)


def reference(stem, branches, mode_order):
    first = contract(stem, branches, mode_order, 0)
    view_two = first.reshape(2, NG, NM, ROWS, NM, U2).transpose(0, 1, 4, 3, 2, 5).reshape(2, NG, NM, ROWS, BLOCK)
    second = contract(view_two, branches, mode_order, 1)
    view_three = second.reshape(2, NG, NM, ROWS, NG, U3).transpose(0, 4, 2, 3, 1, 5).reshape(2, NG, NM, ROWS, BLOCK)
    return contract(view_three, branches, mode_order, 2)
```

```python
import functools

import jax
import jax.numpy as jnp
from jax import lax
from jax.experimental import pallas as pl
from jax.experimental.pallas import tpu as pltpu
from jax.sharding import PartitionSpec as P

BF16 = jnp.bfloat16
F32 = jnp.float32
VMEM_LIMIT = 16 * 1024 * 1024
ROW_SPLIT = (4, 4)
PERMUTE_MAX = 8


def iota(shape, dim):
    return lax.broadcasted_iota(jnp.int32, shape, dim)


def dot(a, b, ca, cb):
    return lax.dot_general(a, b, (((ca,), (cb,)), ((), ())), preferred_element_type=F32)


def ids(count, size, me):
    return size if me is None else size ^ me


def entry(position, part, me):
    owner = position // (2 * part)
    owner = owner if me is None else owner ^ me
    return (position // part) % 2, owner * part + position % part


def both(branch):
    return jnp.concatenate([branch[0], branch[1]], axis=1)


def chosen(order_row, states, column):
    width = order_row.shape[1]
    pick = (iota((width, column), 0) == states).astype(BF16)
    rows = dot(order_row.astype(BF16), pick, 1, 0)
    return (iota((width, column), 0) == rows.astype(jnp.int32)).astype(BF16)


def first_form(branch, order_row, part, me):
    width = order_row.shape[1]
    hot = (iota((width, width), 0) == order_row).astype(BF16)
    turned = dot(both(branch), hot, 0, 0).astype(BF16)
    real, imag = turned[:width], turned[width:]
    return jnp.concatenate(
        [jnp.concatenate([real, -imag], axis=1), jnp.concatenate([imag, real], axis=1)], axis=0
    )


def second_form(branch, order_row, part_in, me_in, part_out, me_out):
    width = order_row.shape[1]
    full = 2 * width
    comp, states = entry(iota((1, full), 1), part_in, me_in)
    hot = chosen(order_row, states, full)
    turned = dot(both(branch), hot, 0, 0)
    real, imag = turned[:width], turned[width:]
    plain = comp == 0
    form = jnp.concatenate(
        [jnp.where(plain, real, -imag), jnp.where(plain, imag, real)], axis=0
    ).astype(BF16)
    out_comp, out_states = entry(iota((full, 1), 0), part_out, me_out)
    place = (iota((full, full), 1) == out_comp * width + out_states).astype(BF16)
    return dot(place, form, 1, 0).astype(BF16)


def third_form(branch, order_row, part_in, me_in):
    width = order_row.shape[1]
    full = 2 * width
    _, states = entry(iota((1, full), 1), part_in, me_in)
    hot = chosen(order_row, states, full)
    taken = dot(hot, both(branch), 0, 0)
    real, imag = taken[:, :width], taken[:, width:]
    comp, _ = entry(iota((full, 1), 0), part_in, me_in)
    plain = comp == 0
    return jnp.concatenate(
        [jnp.where(plain, real, -imag), jnp.where(plain, imag, real)], axis=1
    ).astype(BF16)


def place_of(axis, relative):
    return lax.axis_index(axis) if relative else None


def first_kernel(lo, rows, part, relative, with_form, *refs):
    if with_form:
        stem_ref, branches_ref, order_ref, form_ref, *rest = refs
        rest, (branch, order, more) = rest[:-3], rest[-3:]
        n_out = len(rest) - 2
    else:
        stem_ref, form_ref, *rest = refs
        n_out = len(rest) - 2
    outs, (held, sem) = rest[:n_out], rest[n_out:]
    copies = [
        pltpu.make_async_copy(stem_ref.at[c, 0, 0, pl.ds(lo, rows)], held.at[c], sem.at[c])
        for c in range(2)
    ]
    if with_form:
        early = [
            pltpu.make_async_copy(order_ref, order, more.at[0]),
            pltpu.make_async_copy(branches_ref.at[0], branch, more.at[1]),
        ]
        for copy in early:
            copy.start()
    for copy in copies:
        copy.start()
    if with_form:
        for copy in early:
            copy.wait()
        form_ref[...] = first_form(branch, order[0:1, :], part, None)
    for copy in copies:
        copy.wait()
    joined = jnp.concatenate([held[0], held[1]], axis=1)
    width = form_ref.shape[0] // 2
    me = place_of("mem", relative)
    for k in range(width // part):
        owner = k if me is None else jnp.bitwise_xor(me, k)
        form = jnp.concatenate(
            [form_ref[pl.ds(pl.multiple_of(c * width + owner * part, part), part), :] for c in range(2)],
            axis=0,
        )
        piece = dot(form, joined, 1, 1).astype(BF16)
        if len(outs) == 1:
            outs[0][k] = piece
        else:
            outs[k][...] = piece


def forms_kernel(part1, rel1, part2, rel2, branches_ref, order_ref, second_ref, third_ref, branch, order, sem):
    copies = [
        pltpu.make_async_copy(order_ref, order, sem.at[0]),
        pltpu.make_async_copy(branches_ref, branch, sem.at[1]),
    ]
    for copy in copies:
        copy.start()
    for copy in copies:
        copy.wait()
    me1, me2 = place_of("mem", rel1), place_of("grp", rel2)
    second_ref[...] = second_form(branch[1], order[1:2, :], part1, me1, part2, me2)
    third_ref[...] = third_form(branch[2], order[2:3, :], part2, me2)


def gathered(refs):
    return jnp.concatenate([r[...].reshape(-1, r.shape[-1]) for r in refs], axis=0)


def second_kernel(n_in, *refs):
    form_ref, ins, outs = refs[0], refs[1 : 1 + n_in], refs[1 + n_in :]
    result = dot(form_ref[...], gathered(ins), 1, 0).astype(BF16)
    if len(outs) == 1:
        outs[0][...] = result
    else:
        size = result.shape[0] // len(outs)
        for k, out in enumerate(outs):
            out[...] = result[k * size : (k + 1) * size]


def third_kernel(n_in, lo, rows, first, *refs):
    form_ref, ins, rest = refs[0], refs[1 : 1 + n_in], refs[1 + n_in :]
    out_ref, held, sem = rest[-3:]
    result = dot(gathered(ins), form_ref[...], 0, 0).astype(BF16)
    width = result.shape[1] // 2
    for c in range(2):
        held[c] = result[:, c * width : (c + 1) * width]
    copies = [
        pltpu.make_async_copy(held.at[c], out_ref.at[c, 0, 0, pl.ds(lo, rows)], sem.at[c])
        for c in range(2)
    ]
    for copy in copies:
        copy.start()
    for copy in copies:
        copy.wait()


ANY = pl.BlockSpec(memory_space=pl.ANY)
HBM = pl.BlockSpec(memory_space=pltpu.HBM)
VM = pl.BlockSpec(memory_space=pltpu.VMEM)


def call(kernel, in_specs, out_shapes, out_specs, flops, moved, scratch=(), aliases={}):
    return pl.pallas_call(
        kernel,
        in_specs=in_specs,
        out_shape=out_shapes,
        out_specs=out_specs,
        scratch_shapes=list(scratch),
        input_output_aliases=aliases,
        compiler_params=pltpu.CompilerParams(vmem_limit_bytes=VMEM_LIMIT),
        cost_estimate=pl.CostEstimate(flops=flops, bytes_accessed=moved, transcendentals=0),
    )


def swap(piece, axis, count, k):
    return lax.ppermute(piece, axis, [(i, i ^ k) for i in range(count)])


def exchange(pieces, axis, count, relative):
    if relative:
        order = sorted(range(1, count), key=lambda k: -k)
        got = {k: swap(pieces[k], axis, count, k) for k in order}
        return [pieces[0]] + [got[k] for k in range(1, count)]
    (whole,) = pieces
    shaped = whole.reshape(count, -1, whole.shape[-1])
    moved = lax.all_to_all(shaped, axis, split_axis=0, concat_axis=0, tiled=True)
    return [moved.reshape(-1, whole.shape[-1])]


def local(stem, branches, mode_order, z_relative=True, g_relative=True):
    row_count, width = stem.shape[3], stem.shape[4]
    full = 2 * width
    inner, outer = lax.axis_size("mem"), lax.axis_size("grp")
    part1, part2 = width // inner, width // outer
    z_relative = z_relative and inner <= PERMUTE_MAX
    g_relative = g_relative and outer <= PERMUTE_MAX
    unit = row_count // sum(ROW_SPLIT)
    sizes = [unit * s for s in ROW_SPLIT]
    starts = [sum(sizes[:n]) for n in range(len(sizes))]
    form_shape = jax.ShapeDtypeStruct((full, full), BF16)

    def pieces_of(rows, count, relative):
        if relative:
            return [jax.ShapeDtypeStruct((full // count, rows), BF16)] * count
        return [jax.ShapeDtypeStruct((full, rows), BF16)]

    stem, branches, mode_order = (
        pltpu.with_memory_space_constraint(a, pltpu.HBM) for a in (stem, branches, mode_order)
    )
    form0 = None
    sent = []
    for n, (lo, rows) in enumerate(zip(starts, sizes)):
        if z_relative:
            shapes = [jax.ShapeDtypeStruct((full // inner, rows), BF16)] * inner
        else:
            shapes = [jax.ShapeDtypeStruct((inner, full // inner, rows), BF16)]
        kernel = functools.partial(first_kernel, lo, rows, part1, z_relative, n == 0)
        scratch = [pltpu.VMEM((2, rows, width), BF16), pltpu.SemaphoreType.DMA((2,))]
        flops, moved = 1, 1
        if n == 0:
            made = call(
                kernel, [HBM, HBM, HBM], [form_shape] + shapes, [VM] * (1 + len(shapes)), flops, moved,
                scratch + [
                    pltpu.VMEM(branches.shape[1:], BF16),
                    pltpu.VMEM(mode_order.shape, jnp.int32),
                    pltpu.SemaphoreType.DMA((2,)),
                ],
            )(stem, branches, mode_order)
            form0, made = made[0], made[1:]
        else:
            made = call(kernel, [HBM, VM], shapes, [VM] * len(shapes), flops, moved, scratch)(stem, form0)
        sent.append([m.reshape(-1, rows) if not z_relative else m for m in made])
    form1, form2 = call(
        functools.partial(forms_kernel, part1, z_relative, part2, g_relative),
        [HBM, HBM], [form_shape] * 2, [VM] * 2, 1, 1,
        [pltpu.VMEM(branches.shape, BF16), pltpu.VMEM(mode_order.shape, jnp.int32), pltpu.SemaphoreType.DMA((2,))],
    )(branches, mode_order)
    arrived = [exchange(p, "mem", inner, z_relative) for p in sent]
    out = None
    finals = []
    for n, rows in enumerate(sizes):
        ins = arrived[n]
        shapes = pieces_of(rows, outer, g_relative)
        made = call(
            functools.partial(second_kernel, len(ins)), [VM] * (1 + len(ins)), shapes, [VM] * len(shapes),
            *((10**11, 10**8) if n else (1, 1)),
        )(form1, *ins)
        finals.append(exchange(made, "grp", outer, g_relative))
    for n, (lo, rows) in enumerate(zip(starts, sizes)):
        ins = finals[n]
        kernel = functools.partial(third_kernel, len(ins), lo, rows, n == 0)
        scratch = [pltpu.VMEM((2, rows, width), BF16), pltpu.SemaphoreType.DMA((2,))]
        more = [] if out is None else [out]
        out = call(
            kernel, [VM] * (1 + len(ins)) + [ANY] * len(more), jax.ShapeDtypeStruct(stem.shape, BF16), ANY,
            2 * full * full * rows, 4 * full * rows, scratch, {1 + len(ins): 0} if more else {},
        )(form2, *ins, *more)
    return out


def solution(mesh):
    in_specs = (P(None, "grp", "mem", None, None), P(), P())
    out_specs = P(None, "grp", "mem", None, None)
    return jax.shard_map(local, mesh=mesh, in_specs=in_specs, out_specs=out_specs, check_vma=False)
```

```python
import functools

import jax
import jax.numpy as jnp
from jax import lax
from jax.experimental import pallas as pl
from jax.experimental.pallas import tpu as pltpu
from jax.sharding import PartitionSpec as P

BF16 = jnp.bfloat16
F32 = jnp.float32
VMEM_LIMIT = 16 * 1024 * 1024
ROW_SPLIT = (4, 4)
PERMUTE_MAX = 8
STEPPED = (False, True)


def iota(shape, dim):
    return lax.broadcasted_iota(jnp.int32, shape, dim)


def dot(a, b, ca, cb):
    return lax.dot_general(a, b, (((ca,), (cb,)), ((), ())), preferred_element_type=F32)


def ids(count, size, me):
    return size if me is None else size ^ me


def entry(position, part, me):
    owner = position // (2 * part)
    owner = owner if me is None else owner ^ me
    return (position // part) % 2, owner * part + position % part


def both(branch):
    return jnp.concatenate([branch[0], branch[1]], axis=1)


def chosen(order_row, states, column):
    width = order_row.shape[1]
    pick = (iota((width, column), 0) == states).astype(BF16)
    rows = dot(order_row.astype(BF16), pick, 1, 0)
    return (iota((width, column), 0) == rows.astype(jnp.int32)).astype(BF16)


def first_form(branch, order_row, part, me):
    width = order_row.shape[1]
    hot = (iota((width, width), 0) == order_row).astype(BF16)
    turned = dot(both(branch), hot, 0, 0).astype(BF16)
    real, imag = turned[:width], turned[width:]
    return jnp.concatenate(
        [jnp.concatenate([real, -imag], axis=1), jnp.concatenate([imag, real], axis=1)], axis=0
    )


def second_form(branch, order_row, part_in, me_in, part_out, me_out):
    width = order_row.shape[1]
    full = 2 * width
    comp, states = entry(iota((1, full), 1), part_in, me_in)
    hot = chosen(order_row, states, full)
    turned = dot(both(branch), hot, 0, 0)
    real, imag = turned[:width], turned[width:]
    plain = comp == 0
    form = jnp.concatenate(
        [jnp.where(plain, real, -imag), jnp.where(plain, imag, real)], axis=0
    ).astype(BF16)
    out_comp, out_states = entry(iota((full, 1), 0), part_out, me_out)
    place = (iota((full, full), 1) == out_comp * width + out_states).astype(BF16)
    return dot(place, form, 1, 0).astype(BF16)


def third_form(branch, order_row, part_in, me_in):
    width = order_row.shape[1]
    full = 2 * width
    _, states = entry(iota((1, full), 1), part_in, me_in)
    hot = chosen(order_row, states, full)
    taken = dot(hot, both(branch), 0, 0)
    real, imag = taken[:, :width], taken[:, width:]
    comp, _ = entry(iota((full, 1), 0), part_in, me_in)
    plain = comp == 0
    return jnp.concatenate(
        [jnp.where(plain, real, -imag), jnp.where(plain, imag, real)], axis=1
    ).astype(BF16)


def place_of(axis, relative):
    return lax.axis_index(axis) if relative else None


def first_pieces(form_ref, block, part, me):
    width = block.shape[2]
    form = []
    for k in range(width // part):
        owner = k if me is None else jnp.bitwise_xor(me, k)
        form += [form_ref[pl.ds(pl.multiple_of(c * width + owner * part, part), part), :] for c in range(2)]
    joined = jnp.concatenate([block[0], block[1]], axis=1)
    result = dot(jnp.concatenate(form, axis=0), joined, 1, 1).astype(BF16)
    return [result[2 * part * k : 2 * part * (k + 1)] for k in range(width // part)]


def put(pieces, outs):
    if len(outs) == 1 and len(pieces) > 1:
        outs[0][...] = jnp.concatenate(pieces, axis=0)
    else:
        for piece, out in zip(pieces, outs):
            out[...] = piece


def opening_kernel(rows, part, relative, stem_ref, branches_ref, order_ref, form_ref, *rest):
    outs, (branch, order, block, sem) = rest[:-4], rest[-4:]
    copies = [
        pltpu.make_async_copy(order_ref, order, sem.at[0]),
        pltpu.make_async_copy(branches_ref.at[0], branch, sem.at[1]),
        pltpu.make_async_copy(stem_ref.at[:, 0, 0, pl.ds(0, rows)], block, sem.at[2]),
    ]
    for copy in copies:
        copy.start()
    copies[0].wait()
    copies[1].wait()
    form_ref[...] = first_form(branch, order[0:1, :], part, None)
    copies[2].wait()
    put(first_pieces(form_ref, block, part, place_of("mem", relative)), outs)


def first_kernel(part, relative, n_out, block_ref, form_ref, *rest):
    put(first_pieces(form_ref, block_ref, part, place_of("mem", relative)), rest[-n_out:])


def forms_kernel(sizes, part1, rel1, part2, rel2, stem_ref, branches_ref, order_ref, second_ref, third_ref, *rest):
    blocks, (branch, order, sem) = rest[:-3], rest[-3:]
    copies = [
        pltpu.make_async_copy(order_ref, order, sem.at[0]),
        pltpu.make_async_copy(branches_ref.at[pl.ds(1, 2)], branch, sem.at[1]),
    ]
    lo = sizes[0]
    for n, rows in enumerate(sizes[1:]):
        copies.append(pltpu.make_async_copy(stem_ref.at[:, 0, 0, pl.ds(lo, rows)], blocks[n], sem.at[2 + n]))
        lo += rows
    for copy in copies:
        copy.start()
    copies[0].wait()
    copies[1].wait()
    me1, me2 = place_of("mem", rel1), place_of("grp", rel2)
    second_ref[...] = second_form(branch[0], order[1:2, :], part1, me1, part2, me2)
    third_ref[...] = third_form(branch[1], order[2:3, :], part2, me2)
    for copy in copies[2:]:
        copy.wait()


def gathered(refs):
    return jnp.concatenate([r[...].reshape(-1, r.shape[-1]) for r in refs], axis=0)


def second_kernel(n_in, count, relative, form_ref, *refs):
    ins, outs = refs[:n_in], refs[n_in:]
    result = dot(form_ref[...], gathered(ins), 1, 0).astype(BF16)
    size = result.shape[0] // count
    if not relative:
        outs[0][...] = result
        return
    me = lax.axis_index("grp")
    for k in range(count):
        block = result[size * k : size * (k + 1)]
        if len(outs) == 1:
            outs[0][pl.ds(pl.multiple_of(jnp.bitwise_xor(me, k) * size, size), size)] = block
        else:
            outs[k % 2][size * (k // 2) : size * (k // 2 + 1)] = block


def merge_kernel(size, count, kept_ref, came_ref, *outs):
    outs = outs[-count:]
    for q, out in enumerate(outs, 1):
        out[:size] = kept_ref[q * size : (q + 1) * size]
        out[size:] = came_ref[q * size : (q + 1) * size]


def third_kernel(n_in, count, relative, lo, rows, form_ref, *refs):
    ins, (out_ref, held, sem) = refs[:n_in], refs[-3:]
    size = form_ref.shape[0] // count
    if n_in > 1:
        ins = (ins[0].at[:size], ins[1].at[:size]) + ins[2:]
    elif relative:
        me = lax.axis_index("grp")
        ins = [ins[0].at[pl.ds(pl.multiple_of(jnp.bitwise_xor(me, k) * size, size), size)] for k in range(count)]
    result = dot(gathered(ins), form_ref[...], 0, 0).astype(BF16)
    width = result.shape[1] // 2
    for c in range(2):
        held[c] = result[:, c * width : (c + 1) * width]
    copies = [
        pltpu.make_async_copy(held.at[c], out_ref.at[c, 0, 0, pl.ds(lo, rows)], sem.at[c])
        for c in range(2)
    ]
    for copy in copies:
        copy.start()
    for copy in copies:
        copy.wait()


ANY = pl.BlockSpec(memory_space=pl.ANY)
HBM = pl.BlockSpec(memory_space=pltpu.HBM)
VM = pl.BlockSpec(memory_space=pltpu.VMEM)


def call(kernel, in_specs, out_shapes, out_specs, flops, moved, scratch=(), aliases={}):
    return pl.pallas_call(
        kernel,
        in_specs=in_specs,
        out_shape=out_shapes,
        out_specs=out_specs,
        scratch_shapes=list(scratch),
        input_output_aliases=aliases,
        compiler_params=pltpu.CompilerParams(vmem_limit_bytes=VMEM_LIMIT),
        cost_estimate=pl.CostEstimate(flops=flops, bytes_accessed=moved, transcendentals=0),
    )


def swap(piece, axis, count, k):
    return lax.ppermute(piece, axis, [(i, i ^ k) for i in range(count)])


def whole_exchange(whole, axis, count):
    shaped = whole.reshape(count, -1, whole.shape[-1])
    moved = lax.all_to_all(shaped, axis, split_axis=0, concat_axis=0, tiled=True)
    return [moved.reshape(-1, whole.shape[-1])]


def shape(*dims):
    return jax.ShapeDtypeStruct(dims, BF16)


def plain(count):
    return count > PERMUTE_MAX or count < 4 or count & (count - 1) != 0


def local(stem, branches, mode_order):
    row_count, width = stem.shape[3], stem.shape[4]
    full = 2 * width
    inner, outer = lax.axis_size("mem"), lax.axis_size("grp")
    part1, part2 = width // inner, width // outer
    rel1, rel2 = not plain(inner), not plain(outer)
    unit = row_count // sum(ROW_SPLIT)
    sizes = [unit * s for s in ROW_SPLIT]
    starts = [sum(sizes[:n]) for n in range(len(sizes))]
    stem, branches, mode_order = (
        pltpu.with_memory_space_constraint(a, pltpu.HBM) for a in (stem, branches, mode_order)
    )
    form_shape = shape(full, full)

    def first_shapes(rows):
        return [shape(full // inner, rows)] * inner if rel1 else [shape(full, rows)]

    form0, *pieces = call(
        functools.partial(opening_kernel, sizes[0], part1, rel1),
        [HBM] * 3, [form_shape] + first_shapes(sizes[0]), [VM] * (1 + len(first_shapes(sizes[0]))), *COST["open"],
        [
            pltpu.VMEM(branches.shape[1:], BF16),
            pltpu.VMEM(mode_order.shape, jnp.int32),
            pltpu.VMEM((2, sizes[0], width), BF16),
            pltpu.SemaphoreType.DMA((3,)),
        ],
    )(stem, branches, mode_order)
    form1, form2, *blocks = call(
        functools.partial(forms_kernel, sizes, part1, rel1, part2, rel2),
        [HBM] * 3, [form_shape] * 2 + [shape(2, rows, width) for rows in sizes[1:]], [VM] * (1 + len(sizes)),
        *COST["forms"],
        [
            pltpu.VMEM((2,) + branches.shape[1:], BF16),
            pltpu.VMEM(mode_order.shape, jnp.int32),
            pltpu.SemaphoreType.DMA((1 + len(sizes),)),
        ],
    )(stem, branches, mode_order)

    arrived = []
    for n, rows in enumerate(sizes):
        if n:
            wait = FIRST_AFTER(arrived, form1) if rel1 else []
            shapes = first_shapes(rows)
            pieces = call(
                functools.partial(first_kernel, part1, rel1, len(shapes)),
                [VM, VM] + [ANY] * len(wait), shapes, [VM] * len(shapes), *COST["first"],
            )(blocks[n - 1], form0, *wait)
        if rel1:
            got = {k: swap(pieces[k], "mem", inner, k) for k in range(1, inner)}
            arrived.append([pieces[0]] + [got[k] for k in range(1, inner)])
        else:
            arrived.append(whole_exchange(pieces[0], "mem", inner))

    out = None
    for n, (lo, rows) in enumerate(zip(starts, sizes)):
        ins = arrived[n]
        stepped = rel2 and STEPPED[n]
        shapes = [shape(full // 2, rows)] * 2 if stepped else [shape(full, rows)]
        made = call(
            functools.partial(second_kernel, len(ins), outer, rel2),
            [VM] * (1 + len(ins)), shapes, [VM] * len(shapes), *COST["second"][n],
        )(form1, *ins)
        if stepped:
            kept, given = made
            came = swap(given, "grp", outer, 1)
            pairs = outer // 2
            merged = call(
                functools.partial(merge_kernel, full // outer, pairs - 1),
                [VM] * 2, [shape(full // pairs, rows)] * (pairs - 1), [VM] * (pairs - 1), *COST["merge"],
            )(kept, came)
            got = {q: swap(merged[q - 1], "grp", outer, 2 * q) for q in range(1, pairs)}
            ins = [kept, came] + [got[q] for q in range(1, pairs)]
        else:
            ins = whole_exchange(made[0], "grp", outer)
        more = [] if out is None else [out]
        out = call(
            functools.partial(third_kernel, len(ins), outer, rel2, lo, rows),
            [VM] * (1 + len(ins)) + [ANY] * len(more), shape(*stem.shape), ANY, *COST["third"],
            [pltpu.VMEM((2, rows, width), BF16), pltpu.SemaphoreType.DMA((2,))],
            {1 + len(ins): 0} if more else {},
        )(form2, *ins, *more)
    return out


def FIRST_AFTER(arrived, form1):
    return [arrived[-1][2], form1]


COST = {
    "open": (1, 1),
    "forms": (1, 1),
    "first": (1, 1),
    "second": [(1, 1), (10**11, 10**8)],
    "merge": (1, 1),
    "third": (1, 1),
}


def solution(mesh):
    in_specs = (P(None, "grp", "mem", None, None), P(), P())
    out_specs = P(None, "grp", "mem", None, None)
    return jax.shard_map(local, mesh=mesh, in_specs=in_specs, out_specs=out_specs, check_vma=False)
```

```python
import functools

import jax
import jax.numpy as jnp
from jax import lax
from jax.experimental import pallas as pl
from jax.experimental.pallas import tpu as pltpu
from jax.sharding import PartitionSpec as P

BF16 = jnp.bfloat16
F32 = jnp.float32
VMEM_LIMIT = 16 * 1024 * 1024
ROW_SPLIT = (1, 1)
PERMUTE_MAX = 8
WRITE_CUT = 2
FREE, LONG = 1, 10**11


def iota(shape, dim):
    return lax.broadcasted_iota(jnp.int32, shape, dim)


def dot(a, b, ca, cb):
    return lax.dot_general(a, b, (((ca,), (cb,)), ((), ())), preferred_element_type=F32)


def entry(position, part, me):
    owner = position // (2 * part)
    owner = owner if me is None else owner ^ me
    return (position // part) % 2, owner * part + position % part


def both(branch):
    return jnp.concatenate([branch[0], branch[1]], axis=1)


def chosen(order_row, states, column):
    width = order_row.shape[1]
    pick = (iota((width, column), 0) == states).astype(BF16)
    rows = dot(order_row.astype(BF16), pick, 1, 0)
    return (iota((width, column), 0) == rows.astype(jnp.int32)).astype(BF16)


def first_form(branch, order_row):
    width = order_row.shape[1]
    hot = (iota((width, width), 0) == order_row).astype(BF16)
    taken = dot(both(branch), hot, 0, 0).astype(BF16)
    real, imag = taken[:width], taken[width:]
    return jnp.concatenate(
        [jnp.concatenate([real, -imag], axis=1), jnp.concatenate([imag, real], axis=1)], axis=0
    )


def second_form(branch, order_row, part_in, me_in, part_out, me_out):
    width = order_row.shape[1]
    full = 2 * width
    comp, states = entry(iota((1, full), 1), part_in, me_in)
    hot = chosen(order_row, states, full)
    taken = dot(both(branch), hot, 0, 0)
    real, imag = taken[:width], taken[width:]
    plain = comp == 0
    form = jnp.concatenate(
        [jnp.where(plain, real, -imag), jnp.where(plain, imag, real)], axis=0
    ).astype(BF16)
    out_comp, out_states = entry(iota((full, 1), 0), part_out, me_out)
    place = (iota((full, full), 1) == out_comp * width + out_states).astype(BF16)
    return dot(place, form, 1, 0).astype(BF16)


def third_form(branch, order_row, part_in, me_in):
    width = order_row.shape[1]
    full = 2 * width
    _, states = entry(iota((1, full), 1), part_in, me_in)
    hot = chosen(order_row, states, full)
    taken = dot(hot, both(branch), 0, 0)
    real, imag = taken[:, :width], taken[:, width:]
    comp, _ = entry(iota((full, 1), 0), part_in, me_in)
    plain = comp == 0
    return jnp.concatenate(
        [jnp.where(plain, real, -imag), jnp.where(plain, imag, real)], axis=1
    ).astype(BF16)


def place_of(axis, relative):
    return lax.axis_index(axis) if relative else None


def put_first(form_ref, block, part, me, owners, outs):
    width = block.shape[2]
    form = []
    for k in owners:
        owner = k if me is None else jnp.bitwise_xor(me, k)
        form += [form_ref[pl.ds(pl.multiple_of(c * width + owner * part, part), part), :] for c in range(2)]
    joined = jnp.concatenate([block[0], block[1]], axis=1)
    result = dot(jnp.concatenate(form, axis=0), joined, 1, 1).astype(BF16)
    size = result.shape[0] // len(outs)
    for n, out in enumerate(outs):
        out[...] = result[size * n : size * (n + 1)]


def opening_kernel(part, relative, owners, stem_ref, branches_ref, order_ref, form_ref, block_ref, *rest):
    outs, (branch, order, sem) = rest[:-3], rest[-3:]
    copies = [
        pltpu.make_async_copy(order_ref, order, sem.at[0]),
        pltpu.make_async_copy(branches_ref.at[0], branch, sem.at[1]),
        pltpu.make_async_copy(stem_ref.at[:, 0, 0, pl.ds(0, block_ref.shape[1])], block_ref, sem.at[2]),
    ]
    for copy in copies:
        copy.start()
    copies[0].wait()
    copies[1].wait()
    form_ref[...] = first_form(branch, order[0:1, :])
    copies[2].wait()
    put_first(form_ref, block_ref, part, place_of("mem", relative), owners, outs)


def first_kernel(part, relative, owners, n_out, block_ref, form_ref, *rest):
    put_first(form_ref, block_ref, part, place_of("mem", relative), owners, rest[-n_out:])


def forms_kernel(sizes, part1, rel1, part2, rel2, stem_ref, branches_ref, order_ref, second_ref, third_ref, *rest):
    blocks, (branch, order, sem) = rest[:-3], rest[-3:]
    copies = [
        pltpu.make_async_copy(order_ref, order, sem.at[0]),
        pltpu.make_async_copy(branches_ref.at[pl.ds(1, 2)], branch, sem.at[1]),
    ]
    lo = sizes[0]
    for n, rows in enumerate(sizes[1:]):
        copies.append(pltpu.make_async_copy(stem_ref.at[:, 0, 0, pl.ds(lo, rows)], blocks[n], sem.at[2 + n]))
        lo += rows
    for copy in copies:
        copy.start()
    copies[0].wait()
    copies[1].wait()
    me1, me2 = place_of("mem", rel1), place_of("grp", rel2)
    second_ref[...] = second_form(branch[0], order[1:2, :], part1, me1, part2, me2)
    third_ref[...] = third_form(branch[1], order[2:3, :], part2, me2)
    for copy in copies[2:]:
        copy.wait()


def gathered(refs):
    return jnp.concatenate([ref[...] for ref in refs], axis=0)


def second_kernel(n_in, slots, form_ref, *refs):
    ins, outs = refs[:n_in], refs[n_in:]
    joined = gathered(ins)
    for slot, out in zip(slots, outs):
        rows = out.shape[0]
        out[...] = dot(form_ref[rows * slot : rows * (slot + 1)], joined, 1, 0).astype(BF16)


def pass_kernel(*refs):
    size = refs[0].shape[0] // 2
    for slot, ref in enumerate(refs[:-1]):
        refs[-1][slot * size : (slot + 1) * size] = ref[size:]


def third_kernel(n_in, lo, form_ref, *refs):
    ins, (out_ref, held, sem) = refs[:n_in], refs[-3:]
    if n_in > 1:
        size = ins[0].shape[0] // 2
        ins = sum(
            [[ref.at[:size], ins[-1].at[slot * size : (slot + 1) * size]] for slot, ref in enumerate(ins[:-1])], []
        )
    joined, form = gathered(ins), form_ref[...]
    width, rows = form.shape[1] // 2, held.shape[1]
    cut = rows // WRITE_CUT
    copies = []
    for n in range(WRITE_CUT):
        result = dot(joined[:, n * cut : (n + 1) * cut], form, 0, 0).astype(BF16)
        for c in range(2):
            held[c, n * cut : (n + 1) * cut] = result[:, c * width : (c + 1) * width]
            there = out_ref.at[c, 0, 0, pl.ds(lo + n * cut, cut)]
            copies.append(pltpu.make_async_copy(held.at[c, pl.ds(n * cut, cut)], there, sem.at[2 * n + c]))
            copies[-1].start()
    for copy in copies:
        copy.wait()


ANY = pl.BlockSpec(memory_space=pl.ANY)
HBM = pl.BlockSpec(memory_space=pltpu.HBM)
VM = pl.BlockSpec(memory_space=pltpu.VMEM)


def call(kernel, in_specs, out_shapes, out_specs, cost=FREE, scratch=(), aliases={}):
    return pl.pallas_call(
        kernel,
        in_specs=in_specs,
        out_shape=out_shapes,
        out_specs=out_specs,
        scratch_shapes=list(scratch),
        input_output_aliases=aliases,
        compiler_params=pltpu.CompilerParams(vmem_limit_bytes=VMEM_LIMIT),
        cost_estimate=pl.CostEstimate(flops=cost, bytes_accessed=max(1, cost // 1000), transcendentals=0),
    )


def swap(piece, axis, count, k):
    return lax.ppermute(piece, axis, [(i, i ^ k) for i in range(count)])


def whole_exchange(whole, axis, count):
    shaped = whole.reshape(count, -1, whole.shape[-1])
    moved = lax.all_to_all(shaped, axis, split_axis=0, concat_axis=0, tiled=True)
    return moved.reshape(whole.shape)


def shape(*dims):
    return jax.ShapeDtypeStruct(dims, BF16)


def by_permutes(count):
    return 4 <= count <= PERMUTE_MAX and count & (count - 1) == 0


def local(stem, branches, mode_order):
    row_count, width = stem.shape[3], stem.shape[4]
    full = 2 * width
    inner, outer = lax.axis_size("mem"), lax.axis_size("grp")
    part1, part2 = width // inner, width // outer
    rel1, rel2 = by_permutes(inner), by_permutes(outer)
    sizes = [row_count * share // sum(ROW_SPLIT) for share in ROW_SPLIT]
    starts = [sum(sizes[:n]) for n in range(len(sizes))]
    last = len(sizes) - 1
    stem, branches, mode_order = (
        pltpu.with_memory_space_constraint(a, pltpu.HBM) for a in (stem, branches, mode_order)
    )
    form_shape = shape(full, full)
    order_scratch = pltpu.VMEM(mode_order.shape, jnp.int32)
    half = inner // 2

    def first_shapes(rows, owners):
        return [shape(full // inner, rows)] * len(owners) if rel1 else [shape(full, rows)]

    def first_pieces(block, owners, after=()):
        shapes = first_shapes(block.shape[1], owners)
        made = call(
            functools.partial(first_kernel, part1, rel1, owners, len(shapes)),
            [VM, VM] + [ANY] * len(after), shapes, [VM] * len(shapes),
        )(block, form0, *after)
        return dict(zip(owners, made))

    def inner_exchange(pieces):
        if not rel1:
            return [whole_exchange(pieces[0], "mem", inner)]
        return [pieces[0]] + [swap(pieces[k], "mem", inner, k) for k in range(1, inner)]

    everything = tuple(range(inner))
    opening = (half,) if rel1 else everything
    shapes = first_shapes(sizes[0], opening)
    form0, block, *made = call(
        functools.partial(opening_kernel, part1, rel1, opening),
        [HBM] * 3, [form_shape, shape(2, sizes[0], width)] + shapes, [VM] * (2 + len(shapes)), FREE,
        [pltpu.VMEM(branches.shape[1:], BF16), order_scratch, pltpu.SemaphoreType.DMA((3,))],
    )(stem, branches, mode_order)
    pieces = dict(zip(opening, made))
    if rel1:
        pieces.update(first_pieces(block, tuple(k for k in everything if k != half)))
    arrived = [inner_exchange(pieces)]
    form1, form2, *blocks = call(
        functools.partial(forms_kernel, sizes, part1, rel1, part2, rel2),
        [HBM] * 3, [form_shape] * 2 + [shape(2, rows, width) for rows in sizes[1:]], [VM] * (1 + len(sizes)), FREE,
        [pltpu.VMEM((2,) + branches.shape[1:], BF16), order_scratch, pltpu.SemaphoreType.DMA((1 + len(sizes),))],
    )(stem, branches, mode_order)
    for block in blocks:
        after = (form1, arrived[-1][half]) if rel1 else ()
        arrived.append(inner_exchange(first_pieces(block, everything, after)))

    pairs = outer // 2

    def second(n, slots, rows_each, cost):
        ins = arrived[n]
        shapes = [shape(rows_each, sizes[n])] * len(slots)
        made = call(
            functools.partial(second_kernel, len(ins), slots), [VM] * (1 + len(ins)), shapes, [VM] * len(slots), cost
        )(form1, *ins)
        return dict(zip(slots, made))

    def outer_exchange(n):
        cost = LONG if n == last else FREE
        if not rel2:
            return [whole_exchange(second(n, (0,), full, cost)[0], "grp", outer)]
        slots = tuple(range(pairs))
        early = slots[:1] + slots[2:] if n == last else slots
        made = second(n, early, full // pairs, cost)
        if n == last:
            made.update(second(n, slots[1:2], full // pairs, FREE))
        came = [made[0]] + [swap(made[q], "grp", outer, 2 * q) for q in slots[1:]]
        passed = call(pass_kernel, [VM] * pairs, shape(full // 2, sizes[n]), VM)(*came)
        return came + [swap(passed, "grp", outer, 1)]

    out = ()
    for n, rows in enumerate(sizes):
        ins = outer_exchange(n)
        out = (
            call(
                functools.partial(third_kernel, len(ins), starts[n]),
                [VM] * (1 + len(ins)) + [ANY] * len(out), shape(*stem.shape), ANY, FREE,
                [pltpu.VMEM((2, rows, width), BF16), pltpu.SemaphoreType.DMA((2 * WRITE_CUT,))],
                {1 + len(ins): 0} if out else {},
            )(form2, *ins, *out),
        )
    return out[0]


def solution(mesh):
    in_specs = (P(None, "grp", "mem", None, None), P(), P())
    out_specs = P(None, "grp", "mem", None, None)
    return jax.shard_map(local, mesh=mesh, in_specs=in_specs, out_specs=out_specs, check_vma=False)
```

```python
import functools

import jax
import jax.numpy as jnp
from jax import lax
from jax.experimental import pallas as pl
from jax.experimental.pallas import tpu as pltpu
from jax.sharding import PartitionSpec as P

BF16 = jnp.bfloat16
F32 = jnp.float32
VMEM_LIMIT = 16 * 1024 * 1024
ROW_SPLIT = (1, 1)
PERMUTE_MAX = 8
WRITE_CUT = 2
FREE, LONG = 1, 10**11


def iota(shape, dim):
    return lax.broadcasted_iota(jnp.int32, shape, dim)


def dot(a, b, ca, cb):
    return lax.dot_general(a, b, (((ca,), (cb,)), ((), ())), preferred_element_type=F32)


def entry(position, part, me):
    owner = position // (2 * part)
    owner = owner if me is None else owner ^ me
    return (position // part) % 2, owner * part + position % part


def both(branch):
    return jnp.concatenate([branch[0], branch[1]], axis=1)


def chosen(order_row, states, column):
    width = order_row.shape[1]
    pick = (iota((width, column), 0) == states).astype(BF16)
    rows = dot(order_row.astype(BF16), pick, 1, 0)
    return (iota((width, column), 0) == rows.astype(jnp.int32)).astype(BF16)


def first_form(branch, order_row):
    width = order_row.shape[1]
    hot = (iota((width, width), 0) == order_row).astype(BF16)
    taken = dot(both(branch), hot, 0, 0).astype(BF16)
    real, imag = taken[:width], taken[width:]
    return jnp.concatenate(
        [jnp.concatenate([real, -imag], axis=1), jnp.concatenate([imag, real], axis=1)], axis=0
    )


def second_form(branch, order_row, part_in, me_in, part_out, me_out):
    width = order_row.shape[1]
    full = 2 * width
    comp, states = entry(iota((1, full), 1), part_in, me_in)
    hot = chosen(order_row, states, full)
    taken = dot(both(branch), hot, 0, 0)
    real, imag = taken[:width], taken[width:]
    plain = comp == 0
    form = jnp.concatenate(
        [jnp.where(plain, real, -imag), jnp.where(plain, imag, real)], axis=0
    ).astype(BF16)
    out_comp, out_states = entry(iota((full, 1), 0), part_out, me_out)
    place = (iota((full, full), 1) == out_comp * width + out_states).astype(BF16)
    return dot(place, form, 1, 0).astype(BF16)


def third_form(branch, order_row, part_in, me_in):
    width = order_row.shape[1]
    full = 2 * width
    _, states = entry(iota((1, full), 1), part_in, me_in)
    hot = chosen(order_row, states, full)
    taken = dot(hot, both(branch), 0, 0)
    real, imag = taken[:, :width], taken[:, width:]
    comp, _ = entry(iota((full, 1), 0), part_in, me_in)
    plain = comp == 0
    return jnp.concatenate(
        [jnp.where(plain, real, -imag), jnp.where(plain, imag, real)], axis=1
    ).astype(BF16)


def place_of(axis, relative):
    return lax.axis_index(axis) if relative else None


def put_first(form_ref, block, part, me, owners, outs):
    width = block.shape[2]
    form = []
    for k in owners:
        owner = k if me is None else jnp.bitwise_xor(me, k)
        form += [form_ref[pl.ds(pl.multiple_of(c * width + owner * part, part), part), :] for c in range(2)]
    joined = jnp.concatenate([block[0], block[1]], axis=1)
    result = dot(jnp.concatenate(form, axis=0), joined, 1, 1).astype(BF16)
    size = result.shape[0] // len(outs)
    for n, out in enumerate(outs):
        out[...] = result[size * n : size * (n + 1)]


def opening_kernel(part, relative, owners, stem_ref, branches_ref, order_ref, form_ref, block_ref, *rest):
    outs, (branch, order, sem) = rest[:-3], rest[-3:]
    copies = [
        pltpu.make_async_copy(order_ref, order, sem.at[0]),
        pltpu.make_async_copy(branches_ref.at[0], branch, sem.at[1]),
        pltpu.make_async_copy(stem_ref.at[:, 0, 0, pl.ds(0, block_ref.shape[1])], block_ref, sem.at[2]),
    ]
    for copy in copies:
        copy.start()
    copies[0].wait()
    copies[1].wait()
    form_ref[...] = first_form(branch, order[0:1, :])
    copies[2].wait()
    put_first(form_ref, block_ref, part, place_of("mem", relative), owners, outs)


def first_kernel(part, relative, owners, n_out, block_ref, form_ref, *rest):
    put_first(form_ref, block_ref, part, place_of("mem", relative), owners, rest[-n_out:])


def forms_kernel(sizes, part1, rel1, part2, rel2, stem_ref, branches_ref, order_ref, second_ref, third_ref, *rest):
    blocks, (branch, order, sem) = rest[:-3], rest[-3:]
    copies = [
        pltpu.make_async_copy(order_ref, order, sem.at[0]),
        pltpu.make_async_copy(branches_ref.at[pl.ds(1, 2)], branch, sem.at[1]),
    ]
    lo = sizes[0]
    for n, rows in enumerate(sizes[1:]):
        copies.append(pltpu.make_async_copy(stem_ref.at[:, 0, 0, pl.ds(lo, rows)], blocks[n], sem.at[2 + n]))
        lo += rows
    for copy in copies:
        copy.start()
    copies[0].wait()
    copies[1].wait()
    me1, me2 = place_of("mem", rel1), place_of("grp", rel2)
    second_ref[...] = second_form(branch[0], order[1:2, :], part1, me1, part2, me2)
    third_ref[...] = third_form(branch[1], order[2:3, :], part2, me2)
    for copy in copies[2:]:
        copy.wait()


def gathered(refs):
    return jnp.concatenate([ref[...] for ref in refs], axis=0)


def second_kernel(n_in, slots, form_ref, *refs):
    ins, outs = refs[:n_in], refs[n_in:]
    joined = gathered(ins)
    for slot, out in zip(slots, outs):
        rows = out.shape[0]
        out[...] = dot(form_ref[rows * slot : rows * (slot + 1)], joined, 1, 0).astype(BF16)


def pass_kernel(count, *refs):
    size = refs[0].shape[0] // 2
    for slot, ref in enumerate(refs[:count]):
        refs[-1][slot * size : (slot + 1) * size] = ref[size:]


def form_rows(form_ref, size, places):
    return jnp.concatenate([form_ref[size * k : size * (k + 1)] for k in places], axis=0)


def third_part_kernel(places, size, form_ref, *refs):
    joined = jnp.concatenate([ref[:size] for ref in refs[:-1]], axis=0)
    refs[-1][...] = dot(joined, form_rows(form_ref, size, places), 0, 0)


def third_block_kernel(n_in, form_ref, *refs):
    ins, out_ref = refs[:n_in], refs[-1]
    if n_in > 1:
        size = ins[0].shape[0] // 2
        ins = sum(
            [[ref.at[:size], ins[-1].at[slot * size : (slot + 1) * size]] for slot, ref in enumerate(ins[:-1])], []
        )
    result = dot(gathered(ins), form_ref[...], 0, 0).astype(BF16)
    width = out_ref.shape[2]
    for c in range(2):
        out_ref[c] = result[:, c * width : (c + 1) * width]


def closing_kernel(n_done, places, form_ref, *refs):
    done, ins, (out_ref, held, sem) = refs[:n_done], refs[n_done:-3], refs[-3:]
    width, rows = held.shape[2], held.shape[1]
    copies, lo = [], 0

    def write(source, lo, rows):
        copies.append(pltpu.make_async_copy(source, out_ref.at[:, 0, 0, pl.ds(lo, rows)], sem.at[len(copies)]))
        copies[-1].start()

    for ref in done:
        write(ref, lo, ref.shape[1])
        lo += ref.shape[1]
    joined, form = ins[-1][...], form_ref[...]
    if places:
        form = form_rows(form_ref, joined.shape[0] // len(places), places)
    cut = rows // WRITE_CUT
    for at in range(0, rows, cut):
        result = dot(joined[:, at : at + cut], form, 0, 0)
        result = (result + ins[0][at : at + cut] if places else result).astype(BF16)
        for c in range(2):
            held[c, at : at + cut] = result[:, c * width : (c + 1) * width]
        write(held.at[:, pl.ds(at, cut)], lo + at, cut)
    for copy in copies:
        copy.wait()


ANY = pl.BlockSpec(memory_space=pl.ANY)
HBM = pl.BlockSpec(memory_space=pltpu.HBM)
VM = pl.BlockSpec(memory_space=pltpu.VMEM)


def call(kernel, in_specs, out_shapes, out_specs, cost=FREE, scratch=(), aliases={}):
    return pl.pallas_call(
        kernel,
        in_specs=in_specs,
        out_shape=out_shapes,
        out_specs=out_specs,
        scratch_shapes=list(scratch),
        input_output_aliases=aliases,
        compiler_params=pltpu.CompilerParams(vmem_limit_bytes=VMEM_LIMIT),
        cost_estimate=pl.CostEstimate(flops=cost, bytes_accessed=max(1, cost // 1000), transcendentals=0),
    )


def swap(piece, axis, count, k):
    return lax.ppermute(piece, axis, [(i, i ^ k) for i in range(count)])


def whole_exchange(whole, axis, count):
    shaped = whole.reshape(count, -1, whole.shape[-1])
    moved = lax.all_to_all(shaped, axis, split_axis=0, concat_axis=0, tiled=True)
    return moved.reshape(whole.shape)


def shape(*dims):
    return jax.ShapeDtypeStruct(dims, BF16)


def by_permutes(count):
    return 4 <= count <= PERMUTE_MAX and count & (count - 1) == 0


def local(stem, branches, mode_order):
    row_count, width = stem.shape[3], stem.shape[4]
    full = 2 * width
    inner, outer = lax.axis_size("mem"), lax.axis_size("grp")
    part1, part2 = width // inner, width // outer
    rel1, rel2 = by_permutes(inner), by_permutes(outer)
    sizes = [row_count * share // sum(ROW_SPLIT) for share in ROW_SPLIT]
    starts = [sum(sizes[:n]) for n in range(len(sizes))]
    last = len(sizes) - 1
    stem, branches, mode_order = (
        pltpu.with_memory_space_constraint(a, pltpu.HBM) for a in (stem, branches, mode_order)
    )
    form_shape = shape(full, full)
    order_scratch = pltpu.VMEM(mode_order.shape, jnp.int32)
    half = inner // 2

    def first_shapes(rows, owners):
        return [shape(full // inner, rows)] * len(owners) if rel1 else [shape(full, rows)]

    def first_pieces(block, owners, after=()):
        shapes = first_shapes(block.shape[1], owners)
        made = call(
            functools.partial(first_kernel, part1, rel1, owners, len(shapes)),
            [VM, VM] + [ANY] * len(after), shapes, [VM] * len(shapes),
        )(block, form0, *after)
        return dict(zip(owners, made))

    def inner_exchange(pieces):
        if not rel1:
            return [whole_exchange(pieces[0], "mem", inner)]
        return [pieces[0]] + [swap(pieces[k], "mem", inner, k) for k in range(1, inner)]

    everything = tuple(range(inner))
    opening = (half,) if rel1 else everything
    shapes = first_shapes(sizes[0], opening)
    form0, block, *made = call(
        functools.partial(opening_kernel, part1, rel1, opening),
        [HBM] * 3, [form_shape, shape(2, sizes[0], width)] + shapes, [VM] * (2 + len(shapes)), FREE,
        [pltpu.VMEM(branches.shape[1:], BF16), order_scratch, pltpu.SemaphoreType.DMA((3,))],
    )(stem, branches, mode_order)
    pieces = dict(zip(opening, made))
    if rel1:
        pieces.update(first_pieces(block, tuple(k for k in everything if k != half)))
    arrived = [inner_exchange(pieces)]
    form1, form2, *blocks = call(
        functools.partial(forms_kernel, sizes, part1, rel1, part2, rel2),
        [HBM] * 3, [form_shape] * 2 + [shape(2, rows, width) for rows in sizes[1:]], [VM] * (1 + len(sizes)), FREE,
        [pltpu.VMEM((2,) + branches.shape[1:], BF16), order_scratch, pltpu.SemaphoreType.DMA((1 + len(sizes),))],
    )(stem, branches, mode_order)
    for block in blocks:
        after = (form1, arrived[-1][half]) if rel1 else ()
        arrived.append(inner_exchange(first_pieces(block, everything, after)))

    pairs = outer // 2

    def second(n, slots, rows_each, cost):
        ins = arrived[n]
        shapes = [shape(rows_each, sizes[n])] * len(slots)
        made = call(
            functools.partial(second_kernel, len(ins), slots), [VM] * (1 + len(ins)), shapes, [VM] * len(slots), cost
        )(form1, *ins)
        return dict(zip(slots, made))

    def outer_exchange(n):
        if not rel2:
            return [whole_exchange(second(n, (0,), full, LONG if n == last else FREE)[0], "grp", outer)]
        slots = tuple(range(pairs))
        made = second(n, slots, full // pairs, FREE)
        came = [made[0]] + [swap(made[q], "grp", outer, 2 * q) for q in slots[1:]]
        passed = call(functools.partial(pass_kernel, pairs), [VM] * pairs, shape(full // 2, sizes[n]), VM)(*came)
        return came + [swap(passed, "grp", outer, 1)]

    def last_exchange(done):
        slots = (0,) + tuple(range(2, pairs))
        made = second(last, slots, full // pairs, LONG)
        came = {q: swap(made[q], "grp", outer, 2 * q) if q else made[q] for q in slots}
        direct = second(last, (2, 3), full // outer, FREE)
        direct = {k: swap(direct[k], "grp", outer, k) for k in direct}
        passed = call(
            functools.partial(pass_kernel, len(slots)),
            [VM] * len(slots), shape(len(slots) * full // outer, sizes[last]), VM,
        )(*[came[q] for q in slots])
        passed = swap(passed, "grp", outer, 1)
        ins = {2 * q: came[q] for q in slots} | direct
        total = call(
            functools.partial(third_part_kernel, tuple(ins), full // outer),
            [VM] * (1 + len(ins)), jax.ShapeDtypeStruct((sizes[last], full), F32), VM, LONG,
        )(form2, *ins.values())
        return [total, passed], tuple(2 * q + 1 for q in slots)

    done = []
    for n, rows in enumerate(sizes[:-1]):
        ins = outer_exchange(n)
        done.append(
            call(
                functools.partial(third_block_kernel, len(ins)),
                [VM] * (1 + len(ins)), shape(2, rows, width), VM,
            )(form2, *ins)
        )
    ins, places = last_exchange(done) if rel2 else (outer_exchange(last), ())
    return call(
        functools.partial(closing_kernel, last, places),
        [VM] * (1 + last + len(ins)), shape(*stem.shape), ANY, FREE,
        [pltpu.VMEM((2, sizes[-1], width), BF16), pltpu.SemaphoreType.DMA((last + WRITE_CUT,))],
    )(form2, *done, *ins)


def solution(mesh):
    in_specs = (P(None, "grp", "mem", None, None), P(), P())
    out_specs = P(None, "grp", "mem", None, None)
    return jax.shard_map(local, mesh=mesh, in_specs=in_specs, out_specs=out_specs, check_vma=False)
```

```python
import functools

import jax
import jax.numpy as jnp
from jax import lax
from jax.experimental import pallas as pl
from jax.experimental.pallas import tpu as pltpu
from jax.sharding import PartitionSpec as P

BF16 = jnp.bfloat16
F32 = jnp.float32
VMEM_LIMIT = 16 * 1024 * 1024
ROW_SPLIT = (1, 1)
PERMUTE_MAX = 8
WRITE_CUT = 2
FREE, LONG = 1, 10**11


def iota(shape, dim):
    return lax.broadcasted_iota(jnp.int32, shape, dim)


def dot(a, b, ca, cb):
    return lax.dot_general(a, b, (((ca,), (cb,)), ((), ())), preferred_element_type=F32)


def entry(position, part, me):
    owner = position // (2 * part)
    owner = owner if me is None else owner ^ me
    return (position // part) % 2, owner * part + position % part


def both(branch):
    return jnp.concatenate([branch[0], branch[1]], axis=1)


def chosen(order_row, states, column):
    width = order_row.shape[1]
    pick = (iota((width, column), 0) == states).astype(BF16)
    rows = dot(order_row.astype(BF16), pick, 1, 0)
    return (iota((width, column), 0) == rows.astype(jnp.int32)).astype(BF16)


def first_form(branch, order_row):
    width = order_row.shape[1]
    hot = (iota((width, width), 0) == order_row).astype(BF16)
    taken = dot(both(branch), hot, 0, 0).astype(BF16)
    real, imag = taken[:width], taken[width:]
    return jnp.concatenate(
        [jnp.concatenate([real, -imag], axis=1), jnp.concatenate([imag, real], axis=1)], axis=0
    )


def second_form(branch, order_row, part_in, me_in, part_out, me_out):
    width = order_row.shape[1]
    full = 2 * width
    comp, states = entry(iota((1, full), 1), part_in, me_in)
    hot = chosen(order_row, states, full)
    taken = dot(both(branch), hot, 0, 0)
    real, imag = taken[:width], taken[width:]
    plain = comp == 0
    form = jnp.concatenate(
        [jnp.where(plain, real, -imag), jnp.where(plain, imag, real)], axis=0
    ).astype(BF16)
    out_comp, out_states = entry(iota((full, 1), 0), part_out, me_out)
    place = (iota((full, full), 1) == out_comp * width + out_states).astype(BF16)
    return dot(place, form, 1, 0).astype(BF16)


def third_form(branch, order_row, part_in, me_in):
    width = order_row.shape[1]
    full = 2 * width
    _, states = entry(iota((1, full), 1), part_in, me_in)
    hot = chosen(order_row, states, full)
    taken = dot(hot, both(branch), 0, 0)
    real, imag = taken[:, :width], taken[:, width:]
    comp, _ = entry(iota((full, 1), 0), part_in, me_in)
    plain = comp == 0
    return jnp.concatenate(
        [jnp.where(plain, real, -imag), jnp.where(plain, imag, real)], axis=1
    ).astype(BF16)


def place_of(axis, relative):
    return lax.axis_index(axis) if relative else None


def put_first(form_ref, block, part, me, owners, outs):
    width = block.shape[2]
    form = []
    for k in owners:
        owner = k if me is None else jnp.bitwise_xor(me, k)
        form += [form_ref[pl.ds(pl.multiple_of(c * width + owner * part, part), part), :] for c in range(2)]
    joined = jnp.concatenate([block[0], block[1]], axis=1)
    result = dot(jnp.concatenate(form, axis=0), joined, 1, 1).astype(BF16)
    size = result.shape[0] // len(outs)
    for n, out in enumerate(outs):
        out[...] = result[size * n : size * (n + 1)]


def opening_kernel(part, relative, owners, stem_ref, branches_ref, order_ref, form_ref, block_ref, *rest):
    outs, (branch, order, sem) = rest[:-3], rest[-3:]
    copies = [
        pltpu.make_async_copy(order_ref, order, sem.at[0]),
        pltpu.make_async_copy(branches_ref.at[0], branch, sem.at[1]),
        pltpu.make_async_copy(stem_ref.at[:, 0, 0, pl.ds(0, block_ref.shape[1])], block_ref, sem.at[2]),
    ]
    for copy in copies:
        copy.start()
    copies[0].wait()
    copies[1].wait()
    form_ref[...] = first_form(branch, order[0:1, :])
    copies[2].wait()
    put_first(form_ref, block_ref, part, place_of("mem", relative), owners, outs)


def first_kernel(part, relative, owners, n_out, block_ref, form_ref, *rest):
    put_first(form_ref, block_ref, part, place_of("mem", relative), owners, rest[-n_out:])


def forms_kernel(sizes, part1, rel1, part2, rel2, stem_ref, branches_ref, order_ref, second_ref, third_ref, *rest):
    blocks, (branch, order, sem) = rest[:-3], rest[-3:]
    copies = [
        pltpu.make_async_copy(order_ref, order, sem.at[0]),
        pltpu.make_async_copy(branches_ref.at[pl.ds(1, 2)], branch, sem.at[1]),
    ]
    lo = sizes[0]
    for n, rows in enumerate(sizes[1:]):
        copies.append(pltpu.make_async_copy(stem_ref.at[:, 0, 0, pl.ds(lo, rows)], blocks[n], sem.at[2 + n]))
        lo += rows
    for copy in copies:
        copy.start()
    copies[0].wait()
    copies[1].wait()
    me1, me2 = place_of("mem", rel1), place_of("grp", rel2)
    second_ref[...] = second_form(branch[0], order[1:2, :], part1, me1, part2, me2)
    third_ref[...] = third_form(branch[1], order[2:3, :], part2, me2)
    for copy in copies[2:]:
        copy.wait()


def gathered(refs):
    return jnp.concatenate([ref[...] for ref in refs], axis=0)


def second_kernel(n_in, slots, form_ref, *refs):
    ins, outs = refs[:n_in], refs[n_in:]
    joined = gathered(ins)
    for slot, out in zip(slots, outs):
        rows = out.shape[0]
        out[...] = dot(form_ref[rows * slot : rows * (slot + 1)], joined, 1, 0).astype(BF16)


def pass_kernel(count, *refs):
    size = refs[0].shape[0] // 2
    for slot, ref in enumerate(refs[:count]):
        refs[-1][slot * size : (slot + 1) * size] = ref[size:]


def form_rows(form_ref, size, places):
    return jnp.concatenate([form_ref[size * k : size * (k + 1)] for k in places], axis=0)


def third_part_kernel(places, size, form_ref, *refs):
    joined = jnp.concatenate([ref[:size] for ref in refs[: len(places)]], axis=0)
    total = dot(joined, form_rows(form_ref, size, places), 0, 0)
    for before in refs[len(places) : -1]:
        total = total + before[...]
    refs[-1][...] = total


def block_result(places, form_ref, refs, rows):
    joined, form = refs[-1][:, rows], form_ref[...]
    if places:
        form = form_rows(form_ref, joined.shape[0] // len(places), places)
    result = dot(joined, form, 0, 0)
    return (result + refs[0][rows] if places else result).astype(BF16)


def block_kernel(places, form_ref, *refs):
    out_ref = refs[-1]
    width = out_ref.shape[2]
    result = block_result(places, form_ref, refs[:-1], slice(None))
    for c in range(2):
        out_ref[c] = result[:, c * width : (c + 1) * width]


def closing_kernel(n_done, places, form_ref, *refs):
    done, ins, (out_ref, held, sem) = refs[:n_done], refs[n_done:-3], refs[-3:]
    width, rows = held.shape[2], held.shape[1]
    copies, lo = [], 0

    def write(source, at, count):
        copies.append(pltpu.make_async_copy(source, out_ref.at[:, 0, 0, pl.ds(at, count)], sem.at[len(copies)]))
        copies[-1].start()

    for ref in done:
        write(ref, lo, ref.shape[1])
        lo += ref.shape[1]
    cut = rows // WRITE_CUT
    for at in range(0, rows, cut):
        result = block_result(places, form_ref, ins, slice(at, at + cut))
        for c in range(2):
            held[c, at : at + cut] = result[:, c * width : (c + 1) * width]
        write(held.at[:, pl.ds(at, cut)], lo + at, cut)
    for copy in copies:
        copy.wait()


ANY = pl.BlockSpec(memory_space=pl.ANY)
HBM = pl.BlockSpec(memory_space=pltpu.HBM)
VM = pl.BlockSpec(memory_space=pltpu.VMEM)


def call(kernel, in_specs, out_shapes, out_specs, cost=FREE, scratch=(), aliases={}):
    return pl.pallas_call(
        kernel,
        in_specs=in_specs,
        out_shape=out_shapes,
        out_specs=out_specs,
        scratch_shapes=list(scratch),
        input_output_aliases=aliases,
        compiler_params=pltpu.CompilerParams(vmem_limit_bytes=VMEM_LIMIT),
        cost_estimate=pl.CostEstimate(flops=cost, bytes_accessed=max(1, cost // 1000), transcendentals=0),
    )


def swap(piece, axis, count, k):
    return lax.ppermute(piece, axis, [(i, i ^ k) for i in range(count)])


def whole_exchange(whole, axis, count):
    shaped = whole.reshape(count, -1, whole.shape[-1])
    moved = lax.all_to_all(shaped, axis, split_axis=0, concat_axis=0, tiled=True)
    return moved.reshape(whole.shape)


def shape(*dims):
    return jax.ShapeDtypeStruct(dims, BF16)


def by_permutes(count):
    return 4 <= count <= PERMUTE_MAX and count & (count - 1) == 0


def local(stem, branches, mode_order):
    row_count, width = stem.shape[3], stem.shape[4]
    full = 2 * width
    inner, outer = lax.axis_size("mem"), lax.axis_size("grp")
    part1, part2 = width // inner, width // outer
    rel1, rel2 = by_permutes(inner), by_permutes(outer)
    sizes = [row_count * share // sum(ROW_SPLIT) for share in ROW_SPLIT]
    starts = [sum(sizes[:n]) for n in range(len(sizes))]
    last = len(sizes) - 1
    stem, branches, mode_order = (
        pltpu.with_memory_space_constraint(a, pltpu.HBM) for a in (stem, branches, mode_order)
    )
    form_shape = shape(full, full)
    order_scratch = pltpu.VMEM(mode_order.shape, jnp.int32)
    half = inner // 2

    def first_shapes(rows, owners):
        return [shape(full // inner, rows)] * len(owners) if rel1 else [shape(full, rows)]

    def first_pieces(block, owners, after=()):
        shapes = first_shapes(block.shape[1], owners)
        made = call(
            functools.partial(first_kernel, part1, rel1, owners, len(shapes)),
            [VM, VM] + [ANY] * len(after), shapes, [VM] * len(shapes),
        )(block, form0, *after)
        return dict(zip(owners, made))

    def inner_exchange(pieces):
        if not rel1:
            return [whole_exchange(pieces[0], "mem", inner)]
        return [pieces[0]] + [swap(pieces[k], "mem", inner, k) for k in range(1, inner)]

    everything = tuple(range(inner))
    opening = (half,) if rel1 else everything
    shapes = first_shapes(sizes[0], opening)
    form0, block, *made = call(
        functools.partial(opening_kernel, part1, rel1, opening),
        [HBM] * 3, [form_shape, shape(2, sizes[0], width)] + shapes, [VM] * (2 + len(shapes)), FREE,
        [pltpu.VMEM(branches.shape[1:], BF16), order_scratch, pltpu.SemaphoreType.DMA((3,))],
    )(stem, branches, mode_order)
    pieces = dict(zip(opening, made))
    if rel1:
        pieces.update(first_pieces(block, tuple(k for k in everything if k != half)))
    arrived = [inner_exchange(pieces)]
    form1, form2, *blocks = call(
        functools.partial(forms_kernel, sizes, part1, rel1, part2, rel2),
        [HBM] * 3, [form_shape] * 2 + [shape(2, rows, width) for rows in sizes[1:]], [VM] * (1 + len(sizes)), FREE,
        [pltpu.VMEM((2,) + branches.shape[1:], BF16), order_scratch, pltpu.SemaphoreType.DMA((1 + len(sizes),))],
    )(stem, branches, mode_order)
    for block in blocks:
        after = (form1, arrived[-1][half]) if rel1 else ()
        arrived.append(inner_exchange(first_pieces(block, everything, after)))

    pairs = outer // 2

    def second(n, slots, rows_each, cost):
        ins = arrived[n]
        shapes = [shape(rows_each, sizes[n])] * len(slots)
        made = call(
            functools.partial(second_kernel, len(ins), slots), [VM] * (1 + len(ins)), shapes, [VM] * len(slots), cost
        )(form1, *ins)
        return dict(zip(slots, made))

    def third_part(n, blocks, cost, *before):
        return call(
            functools.partial(third_part_kernel, tuple(blocks), full // outer),
            [VM] * (1 + len(blocks) + len(before)), jax.ShapeDtypeStruct((sizes[n], full), F32), VM, cost,
        )(form2, *blocks.values(), *before)

    def pass_on(n, came, after=()):
        given = call(
            functools.partial(pass_kernel, len(came)),
            [VM] * len(came) + [ANY] * len(after), shape(len(came) * full // outer, sizes[n]), VM,
        )(*came.values(), *after)
        return swap(given, "grp", outer, 1), tuple(2 * q + 1 for q in came)

    def outer_exchange(n):
        slots = tuple(range(pairs))
        made = second(n, slots, full // pairs, FREE)
        came = {q: swap(made[q], "grp", outer, 2 * q) if q else made[q] for q in slots}
        total = third_part(n, {2 * q: came[q] for q in slots}, FREE)
        passed, places = pass_on(n, came, (total,))
        return [total, passed], places

    def last_exchange(n):
        slots = (0,) + tuple(range(2, pairs))
        made = second(n, slots[:1], full // pairs, FREE) | second(n, slots[1:], full // pairs, LONG)
        came = {q: swap(made[q], "grp", outer, 2 * q) if q else made[q] for q in slots}
        direct = second(n, (2, 3), full // outer, FREE)
        direct = {k: swap(direct[k], "grp", outer, k) for k in direct}
        passed, places = pass_on(n, came)
        total = third_part(n, {2 * q: came[q] for q in slots}, FREE)
        return [third_part(n, direct, LONG, total), passed], places

    done = []
    for n, rows in enumerate(sizes):
        if not rel2:
            whole = second(n, (0,), full, LONG if n == last else FREE)[0]
            ins, places = [whole_exchange(whole, "grp", outer)], ()
        else:
            ins, places = last_exchange(n) if n == last else outer_exchange(n)
        if n < last:
            kernel = functools.partial(block_kernel, places)
            done.append(call(kernel, [VM] * (1 + len(ins)), shape(2, rows, width), VM)(form2, *ins))
    return call(
        functools.partial(closing_kernel, last, places),
        [VM] * (1 + last + len(ins)), shape(*stem.shape), ANY, FREE,
        [pltpu.VMEM((2, sizes[last], width), BF16), pltpu.SemaphoreType.DMA((last + WRITE_CUT,))],
    )(form2, *done, *ins)


def solution(mesh):
    in_specs = (P(None, "grp", "mem", None, None), P(), P())
    out_specs = P(None, "grp", "mem", None, None)
    return jax.shard_map(local, mesh=mesh, in_specs=in_specs, out_specs=out_specs, check_vma=False)
```

```python
import functools

import jax
import jax.numpy as jnp
from jax import lax
from jax.experimental import pallas as pl
from jax.experimental.pallas import tpu as pltpu
from jax.sharding import PartitionSpec as P

BF16 = jnp.bfloat16
F32 = jnp.float32
VMEM_LIMIT = 16 * 1024 * 1024
ROW_SPLIT = (1, 1)
PERMUTE_MAX = 8
WRITE_CUT = 2
FREE, LONG = 1, 10**11


def iota(shape, dim):
    return lax.broadcasted_iota(jnp.int32, shape, dim)


def dot(a, b, ca, cb):
    return lax.dot_general(a, b, (((ca,), (cb,)), ((), ())), preferred_element_type=F32)


def entry(position, part, me):
    owner = position // (2 * part)
    owner = owner if me is None else owner ^ me
    return (position // part) % 2, owner * part + position % part


def both(branch):
    return jnp.concatenate([branch[0], branch[1]], axis=1)


def chosen(order_row, states, column):
    width = order_row.shape[1]
    pick = (iota((width, column), 0) == states).astype(BF16)
    rows = dot(order_row.astype(BF16), pick, 1, 0)
    return (iota((width, column), 0) == rows.astype(jnp.int32)).astype(BF16)


def first_form(branch, order_row):
    width = order_row.shape[1]
    hot = (iota((width, width), 0) == order_row).astype(BF16)
    taken = dot(both(branch), hot, 0, 0).astype(BF16)
    real, imag = taken[:width], taken[width:]
    return jnp.concatenate(
        [jnp.concatenate([real, -imag], axis=1), jnp.concatenate([imag, real], axis=1)], axis=0
    )


def second_form(branch, order_row, part_in, me_in, part_out, me_out):
    width = order_row.shape[1]
    full = 2 * width
    comp, states = entry(iota((1, full), 1), part_in, me_in)
    hot = chosen(order_row, states, full)
    taken = dot(both(branch), hot, 0, 0)
    real, imag = taken[:width], taken[width:]
    plain = comp == 0
    form = jnp.concatenate(
        [jnp.where(plain, real, -imag), jnp.where(plain, imag, real)], axis=0
    ).astype(BF16)
    out_comp, out_states = entry(iota((full, 1), 0), part_out, me_out)
    place = (iota((full, full), 1) == out_comp * width + out_states).astype(BF16)
    return dot(place, form, 1, 0).astype(BF16)


def third_form(branch, order_row, part_in, me_in):
    width = order_row.shape[1]
    full = 2 * width
    _, states = entry(iota((1, full), 1), part_in, me_in)
    hot = chosen(order_row, states, full)
    taken = dot(hot, both(branch), 0, 0)
    real, imag = taken[:, :width], taken[:, width:]
    comp, _ = entry(iota((full, 1), 0), part_in, me_in)
    plain = comp == 0
    return jnp.concatenate(
        [jnp.where(plain, real, -imag), jnp.where(plain, imag, real)], axis=1
    ).astype(BF16)


def place_of(axis, relative):
    return lax.axis_index(axis) if relative else None


def put_first(form_ref, block, part, me, owners, outs):
    width = block.shape[2]
    form = []
    for k in owners:
        owner = k if me is None else jnp.bitwise_xor(me, k)
        form += [form_ref[pl.ds(pl.multiple_of(c * width + owner * part, part), part), :] for c in range(2)]
    joined = jnp.concatenate([block[0], block[1]], axis=1)
    result = dot(jnp.concatenate(form, axis=0), joined, 1, 1).astype(BF16)
    size = result.shape[0] // len(outs)
    for n, out in enumerate(outs):
        out[...] = result[size * n : size * (n + 1)]


def opening_kernel(part, relative, owners, stem_ref, branches_ref, order_ref, form_ref, block_ref, *rest):
    outs, (branch, order, sem) = rest[:-3], rest[-3:]
    copies = [
        pltpu.make_async_copy(order_ref, order, sem.at[0]),
        pltpu.make_async_copy(branches_ref.at[0], branch, sem.at[1]),
        pltpu.make_async_copy(stem_ref.at[:, 0, 0, pl.ds(0, block_ref.shape[1])], block_ref, sem.at[2]),
    ]
    for copy in copies:
        copy.start()
    copies[0].wait()
    copies[1].wait()
    form_ref[...] = first_form(branch, order[0:1, :])
    copies[2].wait()
    put_first(form_ref, block_ref, part, place_of("mem", relative), owners, outs)


def first_kernel(part, relative, owners, n_out, block_ref, form_ref, *rest):
    put_first(form_ref, block_ref, part, place_of("mem", relative), owners, rest[-n_out:])


def forms_kernel(sizes, part1, rel1, part2, rel2, stem_ref, branches_ref, order_ref, second_ref, third_ref, *rest):
    blocks, (branch, order, sem) = rest[:-3], rest[-3:]
    copies = [
        pltpu.make_async_copy(order_ref, order, sem.at[0]),
        pltpu.make_async_copy(branches_ref.at[pl.ds(1, 2)], branch, sem.at[1]),
    ]
    lo = sizes[0]
    for n, rows in enumerate(sizes[1:]):
        copies.append(pltpu.make_async_copy(stem_ref.at[:, 0, 0, pl.ds(lo, rows)], blocks[n], sem.at[2 + n]))
        lo += rows
    for copy in copies:
        copy.start()
    copies[0].wait()
    copies[1].wait()
    me1, me2 = place_of("mem", rel1), place_of("grp", rel2)
    second_ref[...] = second_form(branch[0], order[1:2, :], part1, me1, part2, me2)
    third_ref[...] = third_form(branch[1], order[2:3, :], part2, me2)
    for copy in copies[2:]:
        copy.wait()


def gathered(refs):
    return jnp.concatenate([ref[...] for ref in refs], axis=0)


def second_kernel(n_in, slots, form_ref, *refs):
    ins, total, outs = refs[:n_in], refs[n_in : -len(slots)], refs[-len(slots) :]
    joined = gathered(ins)
    ahead = form_ref.shape[1] - joined.shape[0]
    for slot, out in zip(slots, outs):
        rows = out.shape[0]
        here = slice(rows * slot, rows * (slot + 1))
        result = dot(form_ref[here, ahead:], joined, 1, 0)
        for before in total:
            result = result + before[here]
        out[...] = result.astype(BF16)


def second_part_kernel(form_ref, *refs):
    joined = gathered(refs[:-1])
    refs[-1][...] = dot(form_ref[:, : joined.shape[0]], joined, 1, 0)


def pass_kernel(count, *refs):
    size = refs[0].shape[0] // 2
    for slot, ref in enumerate(refs[:count]):
        refs[-1][slot * size : (slot + 1) * size] = ref[size:]


def form_rows(form_ref, size, places):
    return jnp.concatenate([form_ref[size * k : size * (k + 1)] for k in places], axis=0)


def third_part_kernel(places, size, form_ref, *refs):
    joined = jnp.concatenate([ref[:size] for ref in refs[: len(places)]], axis=0)
    total = dot(joined, form_rows(form_ref, size, places), 0, 0)
    for before in refs[len(places) : -1]:
        total = total + before[...]
    refs[-1][...] = total


def block_result(places, form_ref, refs, rows):
    joined, form = refs[-1][:, rows], form_ref[...]
    if places:
        form = form_rows(form_ref, joined.shape[0] // len(places), places)
    result = dot(joined, form, 0, 0)
    return (result + refs[0][rows] if places else result).astype(BF16)


def block_kernel(places, form_ref, *refs):
    out_ref = refs[-1]
    width = out_ref.shape[2]
    result = block_result(places, form_ref, refs[:-1], slice(None))
    for c in range(2):
        out_ref[c] = result[:, c * width : (c + 1) * width]


def closing_kernel(n_done, places, form_ref, *refs):
    done, ins, (out_ref, held, sem) = refs[:n_done], refs[n_done:-3], refs[-3:]
    width, rows = held.shape[2], held.shape[1]
    copies, lo = [], 0

    def write(source, at, count):
        copies.append(pltpu.make_async_copy(source, out_ref.at[:, 0, 0, pl.ds(at, count)], sem.at[len(copies)]))
        copies[-1].start()

    for ref in done:
        write(ref, lo, ref.shape[1])
        lo += ref.shape[1]
    cut = rows // WRITE_CUT
    for at in range(0, rows, cut):
        result = block_result(places, form_ref, ins, slice(at, at + cut))
        for c in range(2):
            held[c, at : at + cut] = result[:, c * width : (c + 1) * width]
        write(held.at[:, pl.ds(at, cut)], lo + at, cut)
    for copy in copies:
        copy.wait()


ANY = pl.BlockSpec(memory_space=pl.ANY)
HBM = pl.BlockSpec(memory_space=pltpu.HBM)
VM = pl.BlockSpec(memory_space=pltpu.VMEM)


def call(kernel, in_specs, out_shapes, out_specs, cost=FREE, scratch=(), aliases={}):
    return pl.pallas_call(
        kernel,
        in_specs=in_specs,
        out_shape=out_shapes,
        out_specs=out_specs,
        scratch_shapes=list(scratch),
        input_output_aliases=aliases,
        compiler_params=pltpu.CompilerParams(vmem_limit_bytes=VMEM_LIMIT),
        cost_estimate=pl.CostEstimate(flops=cost, bytes_accessed=max(1, cost // 1000), transcendentals=0),
    )


def swap(piece, axis, count, k):
    return lax.ppermute(piece, axis, [(i, i ^ k) for i in range(count)])


def whole_exchange(whole, axis, count):
    shaped = whole.reshape(count, -1, whole.shape[-1])
    moved = lax.all_to_all(shaped, axis, split_axis=0, concat_axis=0, tiled=True)
    return moved.reshape(whole.shape)


def shape(*dims):
    return jax.ShapeDtypeStruct(dims, BF16)


def by_permutes(count):
    return 4 <= count <= PERMUTE_MAX and count & (count - 1) == 0


def local(stem, branches, mode_order):
    row_count, width = stem.shape[3], stem.shape[4]
    full = 2 * width
    inner, outer = lax.axis_size("mem"), lax.axis_size("grp")
    part1, part2 = width // inner, width // outer
    rel1, rel2 = by_permutes(inner), by_permutes(outer)
    sizes = [row_count * share // sum(ROW_SPLIT) for share in ROW_SPLIT]
    starts = [sum(sizes[:n]) for n in range(len(sizes))]
    last = len(sizes) - 1
    stem, branches, mode_order = (
        pltpu.with_memory_space_constraint(a, pltpu.HBM) for a in (stem, branches, mode_order)
    )
    form_shape = shape(full, full)
    order_scratch = pltpu.VMEM(mode_order.shape, jnp.int32)
    half = inner // 2

    def first_shapes(rows, owners):
        return [shape(full // inner, rows)] * len(owners) if rel1 else [shape(full, rows)]

    def first_pieces(block, owners, after=()):
        shapes = first_shapes(block.shape[1], owners)
        made = call(
            functools.partial(first_kernel, part1, rel1, owners, len(shapes)),
            [VM, VM] + [ANY] * len(after), shapes, [VM] * len(shapes),
        )(block, form0, *after)
        return dict(zip(owners, made))

    def inner_exchange(pieces):
        if not rel1:
            return [whole_exchange(pieces[0], "mem", inner)]
        return [pieces[0]] + [swap(pieces[k], "mem", inner, k) for k in range(1, inner)]

    everything = tuple(range(inner))
    opening = (half,) if rel1 else everything
    shapes = first_shapes(sizes[0], opening)
    form0, block, *made = call(
        functools.partial(opening_kernel, part1, rel1, opening),
        [HBM] * 3, [form_shape, shape(2, sizes[0], width)] + shapes, [VM] * (2 + len(shapes)), FREE,
        [pltpu.VMEM(branches.shape[1:], BF16), order_scratch, pltpu.SemaphoreType.DMA((3,))],
    )(stem, branches, mode_order)
    pieces = dict(zip(opening, made))
    if rel1:
        pieces.update(first_pieces(block, tuple(k for k in everything if k != half)))
    arrived = [inner_exchange(pieces)]
    form1, form2, *blocks = call(
        functools.partial(forms_kernel, sizes, part1, rel1, part2, rel2),
        [HBM] * 3, [form_shape] * 2 + [shape(2, rows, width) for rows in sizes[1:]], [VM] * (1 + len(sizes)), FREE,
        [pltpu.VMEM((2,) + branches.shape[1:], BF16), order_scratch, pltpu.SemaphoreType.DMA((1 + len(sizes),))],
    )(stem, branches, mode_order)
    for block in blocks:
        after = (form1, arrived[-1][half]) if rel1 else ()
        arrived.append(inner_exchange(first_pieces(block, everything, after)))

    pairs = outer // 2

    def second(n, slots, rows_each, cost, total=()):
        ins = arrived[n][half:] if total else arrived[n]
        shapes = [shape(rows_each, sizes[n])] * len(slots)
        made = call(
            functools.partial(second_kernel, len(ins), slots),
            [VM] * (1 + len(ins) + len(total)), shapes, [VM] * len(slots), cost,
        )(form1, *ins, *total)
        return dict(zip(slots, made))

    def third_part(n, blocks, cost, *before):
        return call(
            functools.partial(third_part_kernel, tuple(blocks), full // outer),
            [VM] * (1 + len(blocks) + len(before)), jax.ShapeDtypeStruct((sizes[n], full), F32), VM, cost,
        )(form2, *blocks.values(), *before)

    def pass_on(n, came, after=()):
        given = call(
            functools.partial(pass_kernel, len(came)),
            [VM] * len(came) + [ANY] * len(after), shape(len(came) * full // outer, sizes[n]), VM,
        )(*came.values(), *after)
        return swap(given, "grp", outer, 1), tuple(2 * q + 1 for q in came)

    def outer_exchange(n):
        slots = tuple(range(pairs))
        made = second(n, slots, full // pairs, FREE)
        came = {q: swap(made[q], "grp", outer, 2 * q) if q else made[q] for q in slots}
        total = third_part(n, {2 * q: came[q] for q in slots}, FREE)
        passed, places = pass_on(n, came, (total,))
        return [total, passed], places

    def last_exchange(n):
        slots = (0,) + tuple(range(2, pairs))
        near = ()
        if rel1:
            near = (
                call(
                    second_part_kernel, [VM] * (1 + half), jax.ShapeDtypeStruct((full, sizes[n]), F32), VM, FREE
                )(form1, *arrived[n][:half]),
            )
        made = second(n, slots[:1], full // pairs, FREE, near) | second(n, slots[1:], full // pairs, LONG, near)
        came = {q: swap(made[q], "grp", outer, 2 * q) if q else made[q] for q in slots}
        direct = second(n, (2, 3), full // outer, FREE, near)
        direct = {k: swap(direct[k], "grp", outer, k) for k in direct}
        passed, places = pass_on(n, came)
        total = third_part(n, {2 * q: came[q] for q in slots}, FREE)
        return [third_part(n, direct, LONG, total), passed], places

    done = []
    for n, rows in enumerate(sizes):
        if not rel2:
            whole = second(n, (0,), full, LONG if n == last else FREE)[0]
            ins, places = [whole_exchange(whole, "grp", outer)], ()
        else:
            ins, places = last_exchange(n) if n == last else outer_exchange(n)
        if n < last:
            kernel = functools.partial(block_kernel, places)
            done.append(call(kernel, [VM] * (1 + len(ins)), shape(2, rows, width), VM)(form2, *ins))
    return call(
        functools.partial(closing_kernel, last, places),
        [VM] * (1 + last + len(ins)), shape(*stem.shape), ANY, FREE,
        [pltpu.VMEM((2, sizes[last], width), BF16), pltpu.SemaphoreType.DMA((last + WRITE_CUT,))],
    )(form2, *done, *ins)


def solution(mesh):
    in_specs = (P(None, "grp", "mem", None, None), P(), P())
    out_specs = P(None, "grp", "mem", None, None)
    return jax.shard_map(local, mesh=mesh, in_specs=in_specs, out_specs=out_specs, check_vma=False)
```

```python
import functools

import jax
import jax.numpy as jnp
from jax import lax
from jax.experimental import pallas as pl
from jax.experimental.pallas import tpu as pltpu
from jax.sharding import PartitionSpec as P

BF16 = jnp.bfloat16
F32 = jnp.float32
VMEM_LIMIT = 16 * 1024 * 1024
ROW_SPLIT = (1, 1)
PERMUTE_MAX = 8
WRITE_CUT = 2
FREE, LONG = 1, 10**11


def iota(shape, dim):
    return lax.broadcasted_iota(jnp.int32, shape, dim)


def dot(a, b, ca, cb):
    return lax.dot_general(a, b, (((ca,), (cb,)), ((), ())), preferred_element_type=F32)


def entry(position, part, me):
    owner = position // (2 * part)
    owner = owner if me is None else owner ^ me
    return (position // part) % 2, owner * part + position % part


def both(branch):
    return jnp.concatenate([branch[0], branch[1]], axis=1)


def chosen(order_row, states, column):
    width = order_row.shape[1]
    pick = (iota((width, column), 0) == states).astype(BF16)
    rows = dot(order_row.astype(BF16), pick, 1, 0)
    return (iota((width, column), 0) == rows.astype(jnp.int32)).astype(BF16)


def first_form(branch, order_row):
    width = order_row.shape[1]
    hot = (iota((width, width), 0) == order_row).astype(BF16)
    taken = dot(both(branch), hot, 0, 0).astype(BF16)
    real, imag = taken[:width], taken[width:]
    return jnp.concatenate(
        [jnp.concatenate([real, -imag], axis=1), jnp.concatenate([imag, real], axis=1)], axis=0
    )


def second_form(branch, order_row, part_in, me_in, part_out, me_out):
    width = order_row.shape[1]
    full = 2 * width
    comp, states = entry(iota((1, full), 1), part_in, me_in)
    hot = chosen(order_row, states, full)
    taken = dot(both(branch), hot, 0, 0)
    real, imag = taken[:width], taken[width:]
    plain = comp == 0
    form = jnp.concatenate(
        [jnp.where(plain, real, -imag), jnp.where(plain, imag, real)], axis=0
    ).astype(BF16)
    out_comp, out_states = entry(iota((full, 1), 0), part_out, me_out)
    place = (iota((full, full), 1) == out_comp * width + out_states).astype(BF16)
    return dot(place, form, 1, 0).astype(BF16)


def third_form(branch, order_row, part_in, me_in):
    width = order_row.shape[1]
    full = 2 * width
    _, states = entry(iota((1, full), 1), part_in, me_in)
    hot = chosen(order_row, states, full)
    taken = dot(hot, both(branch), 0, 0)
    real, imag = taken[:, :width], taken[:, width:]
    comp, _ = entry(iota((full, 1), 0), part_in, me_in)
    plain = comp == 0
    return jnp.concatenate(
        [jnp.where(plain, real, -imag), jnp.where(plain, imag, real)], axis=1
    ).astype(BF16)


def place_of(axis, relative):
    return lax.axis_index(axis) if relative else None


def put_first(form_ref, block, part, me, owners, outs):
    width = block.shape[2]
    form = []
    for k in owners:
        owner = k if me is None else jnp.bitwise_xor(me, k)
        form += [form_ref[pl.ds(pl.multiple_of(c * width + owner * part, part), part), :] for c in range(2)]
    joined = jnp.concatenate([block[0], block[1]], axis=1)
    result = dot(jnp.concatenate(form, axis=0), joined, 1, 1).astype(BF16)
    size = result.shape[0] // len(outs)
    for n, out in enumerate(outs):
        out[...] = result[size * n : size * (n + 1)]


def opening_kernel(part, relative, owners, stem_ref, branches_ref, order_ref, form_ref, block_ref, *rest):
    outs, (branch, order, sem) = rest[:-3], rest[-3:]
    copies = [
        pltpu.make_async_copy(order_ref, order, sem.at[0]),
        pltpu.make_async_copy(branches_ref.at[0], branch, sem.at[1]),
        pltpu.make_async_copy(stem_ref.at[:, 0, 0, pl.ds(0, block_ref.shape[1])], block_ref, sem.at[2]),
    ]
    for copy in (copies[1], copies[0], copies[2]):
        copy.start()
    copies[0].wait()
    copies[1].wait()
    form_ref[...] = first_form(branch, order[0:1, :])
    copies[2].wait()
    put_first(form_ref, block_ref, part, place_of("mem", relative), owners, outs)


def first_kernel(part, relative, owners, n_out, block_ref, form_ref, *rest):
    put_first(form_ref, block_ref, part, place_of("mem", relative), owners, rest[-n_out:])


def forms_kernel(sizes, part1, rel1, part2, rel2, stem_ref, branches_ref, order_ref, second_ref, third_ref, *rest):
    blocks, (branch, order, sem) = rest[:-3], rest[-3:]
    copies = [
        pltpu.make_async_copy(order_ref, order, sem.at[0]),
        pltpu.make_async_copy(branches_ref.at[pl.ds(1, 2)], branch, sem.at[1]),
    ]
    lo = sizes[0]
    for n, rows in enumerate(sizes[1:]):
        copies.append(pltpu.make_async_copy(stem_ref.at[:, 0, 0, pl.ds(lo, rows)], blocks[n], sem.at[2 + n]))
        lo += rows
    for copy in copies:
        copy.start()
    copies[0].wait()
    copies[1].wait()
    me1, me2 = place_of("mem", rel1), place_of("grp", rel2)
    second_ref[...] = second_form(branch[0], order[1:2, :], part1, me1, part2, me2)
    third_ref[...] = third_form(branch[1], order[2:3, :], part2, me2)
    for copy in copies[2:]:
        copy.wait()


def gathered(refs):
    return jnp.concatenate([ref[...] for ref in refs], axis=0)


def second_kernel(n_in, slots, form_ref, *refs):
    ins, total, outs = refs[:n_in], refs[n_in : -len(slots)], refs[-len(slots) :]
    joined = gathered(ins)
    ahead = form_ref.shape[1] - joined.shape[0]
    for slot, out in zip(slots, outs):
        rows = out.shape[0]
        here = slice(rows * slot, rows * (slot + 1))
        result = dot(form_ref[here, ahead:], joined, 1, 0)
        for before in total:
            result = result + before[here]
        out[...] = result.astype(BF16)


def second_part_kernel(form_ref, *refs):
    joined = gathered(refs[:-1])
    refs[-1][...] = dot(form_ref[:, : joined.shape[0]], joined, 1, 0)


def pass_kernel(count, *refs):
    size = refs[0].shape[0] // 2
    for slot, ref in enumerate(refs[:count]):
        refs[-1][slot * size : (slot + 1) * size] = ref[size:]


def form_rows(form_ref, size, places):
    return jnp.concatenate([form_ref[size * k : size * (k + 1)] for k in places], axis=0)


def third_part_kernel(places, size, form_ref, *refs):
    joined = jnp.concatenate([ref[:size] for ref in refs[: len(places)]], axis=0)
    total = dot(joined, form_rows(form_ref, size, places), 0, 0)
    for before in refs[len(places) : -1]:
        total = total + before[...]
    refs[-1][...] = total


def block_result(places, form_ref, refs, rows):
    joined, form = refs[-1][:, rows], form_ref[...]
    if places:
        form = form_rows(form_ref, joined.shape[0] // len(places), places)
    result = dot(joined, form, 0, 0)
    return (result + refs[0][rows] if places else result).astype(BF16)


def block_kernel(places, form_ref, *refs):
    out_ref = refs[-1]
    width = out_ref.shape[2]
    result = block_result(places, form_ref, refs[:-1], slice(None))
    for c in range(2):
        out_ref[c] = result[:, c * width : (c + 1) * width]


def closing_kernel(n_done, places, form_ref, *refs):
    done, ins, (out_ref, held, sem) = refs[:n_done], refs[n_done:-3], refs[-3:]
    width, rows = held.shape[2], held.shape[1]
    copies, lo = [], 0

    def write(source, at, count):
        copies.append(pltpu.make_async_copy(source, out_ref.at[:, 0, 0, pl.ds(at, count)], sem.at[len(copies)]))
        copies[-1].start()

    for ref in done:
        write(ref, lo, ref.shape[1])
        lo += ref.shape[1]
    cut = rows // WRITE_CUT
    for at in range(0, rows, cut):
        result = block_result(places, form_ref, ins, slice(at, at + cut))
        for c in range(2):
            held[c, at : at + cut] = result[:, c * width : (c + 1) * width]
        write(held.at[:, pl.ds(at, cut)], lo + at, cut)
    for copy in copies:
        copy.wait()


ANY = pl.BlockSpec(memory_space=pl.ANY)
HBM = pl.BlockSpec(memory_space=pltpu.HBM)
VM = pl.BlockSpec(memory_space=pltpu.VMEM)


def call(kernel, in_specs, out_shapes, out_specs, cost=FREE, scratch=(), aliases={}):
    return pl.pallas_call(
        kernel,
        in_specs=in_specs,
        out_shape=out_shapes,
        out_specs=out_specs,
        scratch_shapes=list(scratch),
        input_output_aliases=aliases,
        compiler_params=pltpu.CompilerParams(vmem_limit_bytes=VMEM_LIMIT),
        cost_estimate=pl.CostEstimate(flops=cost, bytes_accessed=max(1, cost // 1000), transcendentals=0),
    )


def swap(piece, axis, count, k):
    return lax.ppermute(piece, axis, [(i, i ^ k) for i in range(count)])


def whole_exchange(whole, axis, count):
    shaped = whole.reshape(count, -1, whole.shape[-1])
    moved = lax.all_to_all(shaped, axis, split_axis=0, concat_axis=0, tiled=True)
    return moved.reshape(whole.shape)


def shape(*dims):
    return jax.ShapeDtypeStruct(dims, BF16)


def by_permutes(count):
    return 4 <= count <= PERMUTE_MAX and count & (count - 1) == 0


def local(stem, branches, mode_order):
    row_count, width = stem.shape[3], stem.shape[4]
    full = 2 * width
    inner, outer = lax.axis_size("mem"), lax.axis_size("grp")
    part1, part2 = width // inner, width // outer
    rel1, rel2 = by_permutes(inner), by_permutes(outer)
    sizes = [row_count * share // sum(ROW_SPLIT) for share in ROW_SPLIT]
    starts = [sum(sizes[:n]) for n in range(len(sizes))]
    last = len(sizes) - 1
    stem, branches, mode_order = (
        pltpu.with_memory_space_constraint(a, pltpu.HBM) for a in (stem, branches, mode_order)
    )
    form_shape = shape(full, full)
    order_scratch = pltpu.VMEM(mode_order.shape, jnp.int32)
    half = inner // 2

    def first_shapes(rows, owners):
        return [shape(full // inner, rows)] * len(owners) if rel1 else [shape(full, rows)]

    def first_pieces(block, owners, after=()):
        shapes = first_shapes(block.shape[1], owners)
        made = call(
            functools.partial(first_kernel, part1, rel1, owners, len(shapes)),
            [VM, VM] + [ANY] * len(after), shapes, [VM] * len(shapes),
        )(block, form0, *after)
        return dict(zip(owners, made))

    def inner_exchange(pieces):
        if not rel1:
            return [whole_exchange(pieces[0], "mem", inner)]
        return [pieces[0]] + [swap(pieces[k], "mem", inner, k) for k in range(1, inner)]

    everything = tuple(range(inner))
    opening = (half,) if rel1 else everything
    shapes = first_shapes(sizes[0], opening)
    form0, block, *made = call(
        functools.partial(opening_kernel, part1, rel1, opening),
        [HBM] * 3, [form_shape, shape(2, sizes[0], width)] + shapes, [VM] * (2 + len(shapes)), FREE,
        [pltpu.VMEM(branches.shape[1:], BF16), order_scratch, pltpu.SemaphoreType.DMA((3,))],
    )(stem, branches, mode_order)
    pieces = dict(zip(opening, made))
    if rel1:
        pieces.update(first_pieces(block, tuple(k for k in everything if k != half)))
    arrived = [inner_exchange(pieces)]
    form1, form2, *blocks = call(
        functools.partial(forms_kernel, sizes, part1, rel1, part2, rel2),
        [HBM] * 3, [form_shape] * 2 + [shape(2, rows, width) for rows in sizes[1:]], [VM] * (1 + len(sizes)), FREE,
        [pltpu.VMEM((2,) + branches.shape[1:], BF16), order_scratch, pltpu.SemaphoreType.DMA((1 + len(sizes),))],
    )(stem, branches, mode_order)
    for block in blocks:
        after = (form1, arrived[-1][half]) if rel1 else ()
        arrived.append(inner_exchange(first_pieces(block, everything, after)))

    pairs = outer // 2

    def second(n, slots, rows_each, cost, total=()):
        ins = arrived[n][half:] if total else arrived[n]
        shapes = [shape(rows_each, sizes[n])] * len(slots)
        made = call(
            functools.partial(second_kernel, len(ins), slots),
            [VM] * (1 + len(ins) + len(total)), shapes, [VM] * len(slots), cost,
        )(form1, *ins, *total)
        return dict(zip(slots, made))

    def near_sum(n):
        if not rel1:
            return ()
        total = jax.ShapeDtypeStruct((full, sizes[n]), F32)
        return (call(second_part_kernel, [VM] * (1 + half), total, VM)(form1, *arrived[n][:half]),)

    def third_part(n, blocks, cost, *before):
        return call(
            functools.partial(third_part_kernel, tuple(blocks), full // outer),
            [VM] * (1 + len(blocks) + len(before)), jax.ShapeDtypeStruct((sizes[n], full), F32), VM, cost,
        )(form2, *blocks.values(), *before)

    def pass_on(n, came, after=()):
        given = call(
            functools.partial(pass_kernel, len(came)),
            [VM] * len(came) + [ANY] * len(after), shape(len(came) * full // outer, sizes[n]), VM,
        )(*came.values(), *after)
        return swap(given, "grp", outer, 1), tuple(2 * q + 1 for q in came)

    def outer_exchange(n):
        slots = tuple(range(pairs))
        made = second(n, slots, full // pairs, FREE, near_sum(n))
        came = {q: swap(made[q], "grp", outer, 2 * q) if q else made[q] for q in slots}
        total = third_part(n, {2 * q: came[q] for q in slots}, FREE)
        passed, places = pass_on(n, came, (total,))
        return [total, passed], places

    def last_exchange(n):
        slots = (0,) + tuple(range(2, pairs))
        near = near_sum(n)
        made = second(n, slots[:1], full // pairs, FREE, near) | second(n, slots[1:], full // pairs, LONG, near)
        came = {q: swap(made[q], "grp", outer, 2 * q) if q else made[q] for q in slots}
        direct = second(n, (2, 3), full // outer, FREE, near)
        direct = {k: swap(direct[k], "grp", outer, k) for k in direct}
        passed, places = pass_on(n, came)
        total = third_part(n, {2 * q: came[q] for q in slots}, FREE)
        return [third_part(n, direct, LONG, total), passed], places

    done = []
    for n, rows in enumerate(sizes):
        if not rel2:
            whole = second(n, (0,), full, LONG if n == last else FREE)[0]
            ins, places = [whole_exchange(whole, "grp", outer)], ()
        else:
            ins, places = last_exchange(n) if n == last else outer_exchange(n)
        if n < last:
            kernel = functools.partial(block_kernel, places)
            done.append(call(kernel, [VM] * (1 + len(ins)), shape(2, rows, width), VM)(form2, *ins))
    return call(
        functools.partial(closing_kernel, last, places),
        [VM] * (1 + last + len(ins)), shape(*stem.shape), ANY, FREE,
        [pltpu.VMEM((2, sizes[last], width), BF16), pltpu.SemaphoreType.DMA((last + WRITE_CUT,))],
    )(form2, *done, *ins)


def solution(mesh):
    in_specs = (P(None, "grp", "mem", None, None), P(), P())
    out_specs = P(None, "grp", "mem", None, None)
    return jax.shard_map(local, mesh=mesh, in_specs=in_specs, out_specs=out_specs, check_vma=False)
```

```python
import functools

import jax
import jax.numpy as jnp
from jax import lax
from jax.experimental import pallas as pl
from jax.experimental.pallas import tpu as pltpu
from jax.sharding import PartitionSpec as P

BF16 = jnp.bfloat16
F32 = jnp.float32
VMEM_LIMIT = 16 * 1024 * 1024
ROW_SPLIT = (1, 1)
PERMUTE_MAX = 8
WRITE_CUT = 2
FREE, LONG = 1, 10**11


def iota(shape, dim):
    return lax.broadcasted_iota(jnp.int32, shape, dim)


def dot(a, b, ca, cb):
    return lax.dot_general(a, b, (((ca,), (cb,)), ((), ())), preferred_element_type=F32)


def entry(position, part, me):
    owner = position // (2 * part)
    owner = owner if me is None else owner ^ me
    return (position // part) % 2, owner * part + position % part


def both(branch):
    return jnp.concatenate([branch[0], branch[1]], axis=1)


def chosen(order_row, states, column):
    width = order_row.shape[1]
    pick = (iota((width, column), 0) == states).astype(BF16)
    rows = dot(order_row.astype(BF16), pick, 1, 0)
    return (iota((width, column), 0) == rows.astype(jnp.int32)).astype(BF16)


def first_form(branch, order_row):
    width = order_row.shape[1]
    hot = (iota((width, width), 0) == order_row).astype(BF16)
    taken = dot(both(branch), hot, 0, 0).astype(BF16)
    real, imag = taken[:width], taken[width:]
    return jnp.concatenate(
        [jnp.concatenate([real, -imag], axis=1), jnp.concatenate([imag, real], axis=1)], axis=0
    )


def second_form(branch, order_row, part_in, me_in, part_out, me_out):
    width = order_row.shape[1]
    full = 2 * width
    comp, states = entry(iota((1, full), 1), part_in, me_in)
    hot = chosen(order_row, states, full)
    taken = dot(both(branch), hot, 0, 0)
    real, imag = taken[:width], taken[width:]
    plain = comp == 0
    form = jnp.concatenate(
        [jnp.where(plain, real, -imag), jnp.where(plain, imag, real)], axis=0
    ).astype(BF16)
    out_comp, out_states = entry(iota((full, 1), 0), part_out, me_out)
    place = (iota((full, full), 1) == out_comp * width + out_states).astype(BF16)
    return dot(place, form, 1, 0).astype(BF16)


def third_form(branch, order_row, part_in, me_in):
    width = order_row.shape[1]
    full = 2 * width
    _, states = entry(iota((1, full), 1), part_in, me_in)
    hot = chosen(order_row, states, full)
    taken = dot(hot, both(branch), 0, 0)
    real, imag = taken[:, :width], taken[:, width:]
    comp, _ = entry(iota((full, 1), 0), part_in, me_in)
    plain = comp == 0
    return jnp.concatenate(
        [jnp.where(plain, real, -imag), jnp.where(plain, imag, real)], axis=1
    ).astype(BF16)


def place_of(axis, relative):
    return lax.axis_index(axis) if relative else None


def put_first(form_ref, block, part, me, owners, outs):
    width = block.shape[2]
    form = []
    for k in owners:
        owner = k if me is None else jnp.bitwise_xor(me, k)
        form += [form_ref[pl.ds(pl.multiple_of(c * width + owner * part, part), part), :] for c in range(2)]
    joined = jnp.concatenate([block[0], block[1]], axis=1)
    result = dot(jnp.concatenate(form, axis=0), joined, 1, 1).astype(BF16)
    size = result.shape[0] // len(outs)
    for n, out in enumerate(outs):
        out[...] = result[size * n : size * (n + 1)]


def opening_kernel(part, relative, owners, stem_ref, branches_ref, order_ref, form_ref, block_ref, *rest):
    outs, (branch, order, sem) = rest[:-3], rest[-3:]
    copies = [
        pltpu.make_async_copy(order_ref, order, sem.at[0]),
        pltpu.make_async_copy(branches_ref.at[0], branch, sem.at[1]),
        pltpu.make_async_copy(stem_ref.at[:, 0, 0, pl.ds(0, block_ref.shape[1])], block_ref, sem.at[2]),
    ]
    for copy in copies:
        copy.start()
    copies[0].wait()
    copies[1].wait()
    form_ref[...] = first_form(branch, order[0:1, :])
    copies[2].wait()
    put_first(form_ref, block_ref, part, place_of("mem", relative), owners, outs)


def first_kernel(part, relative, owners, n_out, block_ref, form_ref, *rest):
    put_first(form_ref, block_ref, part, place_of("mem", relative), owners, rest[-n_out:])


def forms_kernel(sizes, part1, rel1, part2, rel2, stem_ref, branches_ref, order_ref, second_ref, third_ref, *rest):
    blocks, (branch, order, sem) = rest[:-3], rest[-3:]
    copies = [
        pltpu.make_async_copy(order_ref, order, sem.at[0]),
        pltpu.make_async_copy(branches_ref.at[pl.ds(1, 2)], branch, sem.at[1]),
    ]
    lo = sizes[0]
    for n, rows in enumerate(sizes[1:]):
        copies.append(pltpu.make_async_copy(stem_ref.at[:, 0, 0, pl.ds(lo, rows)], blocks[n], sem.at[2 + n]))
        lo += rows
    for copy in copies:
        copy.start()
    copies[0].wait()
    copies[1].wait()
    me1, me2 = place_of("mem", rel1), place_of("grp", rel2)
    second_ref[...] = second_form(branch[0], order[1:2, :], part1, me1, part2, me2)
    third_ref[...] = third_form(branch[1], order[2:3, :], part2, me2)
    for copy in copies[2:]:
        copy.wait()


def gathered(refs):
    return jnp.concatenate([ref[...] for ref in refs], axis=0)


def second_kernel(n_in, slots, form_ref, *refs):
    ins, total, outs = refs[:n_in], refs[n_in : -len(slots)], refs[-len(slots) :]
    joined = gathered(ins)
    ahead = form_ref.shape[1] - joined.shape[0]
    for slot, out in zip(slots, outs):
        rows = out.shape[0]
        here = slice(rows * slot, rows * (slot + 1))
        result = dot(form_ref[here, ahead:], joined, 1, 0)
        for before in total:
            result = result + before[here]
        out[...] = result.astype(BF16)


def second_part_kernel(form_ref, *refs):
    joined = gathered(refs[:-1])
    refs[-1][...] = dot(form_ref[:, : joined.shape[0]], joined, 1, 0)


def pass_kernel(count, *refs):
    size = refs[0].shape[0] // 2
    for slot, ref in enumerate(refs[:count]):
        refs[-1][slot * size : (slot + 1) * size] = ref[size:]


def form_rows(form_ref, size, places):
    return jnp.concatenate([form_ref[size * k : size * (k + 1)] for k in places], axis=0)


def third_part_kernel(places, size, form_ref, *refs):
    joined = jnp.concatenate([ref[:size] for ref in refs[: len(places)]], axis=0)
    total = dot(joined, form_rows(form_ref, size, places), 0, 0)
    for before in refs[len(places) : -1]:
        total = total + before[...]
    refs[-1][...] = total


def block_result(places, form_ref, refs, rows):
    joined, form = refs[-1][:, rows], form_ref[...]
    if places:
        form = form_rows(form_ref, joined.shape[0] // len(places), places)
    result = dot(joined, form, 0, 0)
    return (result + refs[0][rows] if places else result).astype(BF16)


def block_kernel(places, form_ref, *refs):
    out_ref = refs[-1]
    width = out_ref.shape[2]
    result = block_result(places, form_ref, refs[:-1], slice(None))
    for c in range(2):
        out_ref[c] = result[:, c * width : (c + 1) * width]


def closing_kernel(n_done, places, form_ref, *refs):
    done, ins, (out_ref, held, sem) = refs[:n_done], refs[n_done:-3], refs[-3:]
    width, rows = held.shape[2], held.shape[1]
    copies, lo = [], 0

    def write(source, at, count):
        copies.append(pltpu.make_async_copy(source, out_ref.at[:, 0, 0, pl.ds(at, count)], sem.at[len(copies)]))
        copies[-1].start()

    for ref in done:
        write(ref, lo, ref.shape[1])
        lo += ref.shape[1]
    cut = rows // WRITE_CUT
    for at in range(0, rows, cut):
        result = block_result(places, form_ref, ins, slice(at, at + cut))
        for c in range(2):
            held[c, at : at + cut] = result[:, c * width : (c + 1) * width]
        write(held.at[:, pl.ds(at, cut)], lo + at, cut)
    for copy in copies:
        copy.wait()


ANY = pl.BlockSpec(memory_space=pl.ANY)
HBM = pl.BlockSpec(memory_space=pltpu.HBM)
VM = pl.BlockSpec(memory_space=pltpu.VMEM)


def call(kernel, in_specs, out_shapes, out_specs, cost=FREE, scratch=(), aliases={}):
    return pl.pallas_call(
        kernel,
        in_specs=in_specs,
        out_shape=out_shapes,
        out_specs=out_specs,
        scratch_shapes=list(scratch),
        input_output_aliases=aliases,
        compiler_params=pltpu.CompilerParams(vmem_limit_bytes=VMEM_LIMIT),
        cost_estimate=pl.CostEstimate(flops=cost, bytes_accessed=max(1, cost // 1000), transcendentals=0),
    )


def swap(piece, axis, count, k):
    return lax.ppermute(piece, axis, [(i, i ^ k) for i in range(count)])


def whole_exchange(whole, axis, count):
    shaped = whole.reshape(count, -1, whole.shape[-1])
    moved = lax.all_to_all(shaped, axis, split_axis=0, concat_axis=0, tiled=True)
    return moved.reshape(whole.shape)


def shape(*dims):
    return jax.ShapeDtypeStruct(dims, BF16)


def by_permutes(count):
    return 4 <= count <= PERMUTE_MAX and count & (count - 1) == 0


def local(stem, branches, mode_order):
    row_count, width = stem.shape[3], stem.shape[4]
    full = 2 * width
    inner, outer = lax.axis_size("mem"), lax.axis_size("grp")
    part1, part2 = width // inner, width // outer
    rel1, rel2 = by_permutes(inner), by_permutes(outer)
    sizes = [row_count * share // sum(ROW_SPLIT) for share in ROW_SPLIT]
    starts = [sum(sizes[:n]) for n in range(len(sizes))]
    last = len(sizes) - 1
    stem, branches, mode_order = (
        pltpu.with_memory_space_constraint(a, pltpu.HBM) for a in (stem, branches, mode_order)
    )
    form_shape = shape(full, full)
    order_scratch = pltpu.VMEM(mode_order.shape, jnp.int32)
    half = inner // 2

    def first_shapes(rows, owners):
        return [shape(full // inner, rows)] * len(owners) if rel1 else [shape(full, rows)]

    def first_pieces(block, owners, after=()):
        shapes = first_shapes(block.shape[1], owners)
        made = call(
            functools.partial(first_kernel, part1, rel1, owners, len(shapes)),
            [VM, VM] + [ANY] * len(after), shapes, [VM] * len(shapes),
        )(block, form0, *after)
        return dict(zip(owners, made))

    def inner_exchange(pieces):
        if not rel1:
            return [whole_exchange(pieces[0], "mem", inner)]
        return [pieces[0]] + [swap(pieces[k], "mem", inner, k) for k in range(1, inner)]

    everything = tuple(range(inner))
    opening = (half,) if rel1 else everything
    shapes = first_shapes(sizes[0], opening)
    form0, block, *made = call(
        functools.partial(opening_kernel, part1, rel1, opening),
        [HBM] * 3, [form_shape, shape(2, sizes[0], width)] + shapes, [VM] * (2 + len(shapes)), FREE,
        [pltpu.VMEM(branches.shape[1:], BF16), order_scratch, pltpu.SemaphoreType.DMA((3,))],
    )(stem, branches, mode_order)
    pieces = dict(zip(opening, made))
    if rel1:
        pieces.update(first_pieces(block, tuple(k for k in everything if k != half)))
    arrived = [inner_exchange(pieces)]
    form1, form2, *blocks = call(
        functools.partial(forms_kernel, sizes, part1, rel1, part2, rel2),
        [HBM] * 3, [form_shape] * 2 + [shape(2, rows, width) for rows in sizes[1:]], [VM] * (1 + len(sizes)), FREE,
        [pltpu.VMEM((2,) + branches.shape[1:], BF16), order_scratch, pltpu.SemaphoreType.DMA((1 + len(sizes),))],
    )(stem, branches, mode_order)
    for block in blocks:
        after = (form1, arrived[-1][half]) if rel1 else ()
        arrived.append(inner_exchange(first_pieces(block, everything, after)))

    pairs = outer // 2

    def second(n, slots, rows_each, cost, total=()):
        ins = arrived[n][half:] if total else arrived[n]
        shapes = [shape(rows_each, sizes[n])] * len(slots)
        made = call(
            functools.partial(second_kernel, len(ins), slots),
            [VM] * (1 + len(ins) + len(total)), shapes, [VM] * len(slots), cost,
        )(form1, *ins, *total)
        return dict(zip(slots, made))

    def third_part(n, blocks, cost, *before):
        return call(
            functools.partial(third_part_kernel, tuple(blocks), full // outer),
            [VM] * (1 + len(blocks) + len(before)), jax.ShapeDtypeStruct((sizes[n], full), F32), VM, cost,
        )(form2, *blocks.values(), *before)

    def pass_on(n, came, after=()):
        given = call(
            functools.partial(pass_kernel, len(came)),
            [VM] * len(came) + [ANY] * len(after), shape(len(came) * full // outer, sizes[n]), VM,
        )(*came.values(), *after)
        return swap(given, "grp", outer, 1), tuple(2 * q + 1 for q in came)

    def outer_exchange(n):
        slots = tuple(range(pairs))
        made = second(n, slots, full // pairs, FREE)
        came = {q: swap(made[q], "grp", outer, 2 * q) if q else made[q] for q in slots}
        total = third_part(n, {2 * q: came[q] for q in slots}, FREE)
        passed, places = pass_on(n, came, (total,))
        return [total, passed], places

    def last_exchange(n):
        slots = (0,) + tuple(range(2, pairs))
        near = ()
        if rel1:
            near = (
                call(
                    second_part_kernel, [VM] * (1 + half), jax.ShapeDtypeStruct((full, sizes[n]), F32), VM, FREE
                )(form1, *arrived[n][:half]),
            )
        made = second(n, slots[:1], full // pairs, FREE, near) | second(n, slots[1:], full // pairs, LONG, near)
        came = {q: swap(made[q], "grp", outer, 2 * q) if q else made[q] for q in slots}
        direct = second(n, (2, 3), full // outer, FREE, near)
        direct = {k: swap(direct[k], "grp", outer, k) for k in direct}
        passed, places = pass_on(n, came)
        total = third_part(n, {2 * q: came[q] for q in slots[1:]}, FREE)
        return [third_part(n, {0: came[0]} | direct, LONG, total), passed], places

    done = []
    for n, rows in enumerate(sizes):
        if not rel2:
            whole = second(n, (0,), full, LONG if n == last else FREE)[0]
            ins, places = [whole_exchange(whole, "grp", outer)], ()
        else:
            ins, places = last_exchange(n) if n == last else outer_exchange(n)
        if n < last:
            kernel = functools.partial(block_kernel, places)
            done.append(call(kernel, [VM] * (1 + len(ins)), shape(2, rows, width), VM)(form2, *ins))
    return call(
        functools.partial(closing_kernel, last, places),
        [VM] * (1 + last + len(ins)), shape(*stem.shape), ANY, FREE,
        [pltpu.VMEM((2, sizes[last], width), BF16), pltpu.SemaphoreType.DMA((last + WRITE_CUT,))],
    )(form2, *done, *ins)


def solution(mesh):
    in_specs = (P(None, "grp", "mem", None, None), P(), P())
    out_specs = P(None, "grp", "mem", None, None)
    return jax.shard_map(local, mesh=mesh, in_specs=in_specs, out_specs=out_specs, check_vma=False)
```

```python
import functools

import jax
import jax.numpy as jnp
from jax import lax
from jax.experimental import pallas as pl
from jax.experimental.pallas import tpu as pltpu
from jax.sharding import PartitionSpec as P

BF16 = jnp.bfloat16
F32 = jnp.float32
VMEM_LIMIT = 16 * 1024 * 1024
ROW_SPLIT = (1, 1)
PERMUTE_MAX = 8
WRITE_CUT = 2
FREE, LONG = 1, 10**11


def iota(shape, dim):
    return lax.broadcasted_iota(jnp.int32, shape, dim)


def dot(a, b, ca, cb):
    return lax.dot_general(a, b, (((ca,), (cb,)), ((), ())), preferred_element_type=F32)


def entry(position, part, me):
    owner = position // (2 * part)
    owner = owner if me is None else owner ^ me
    return (position // part) % 2, owner * part + position % part


def both(branch):
    return jnp.concatenate([branch[0], branch[1]], axis=1)


def chosen(order_row, states, column):
    width = order_row.shape[1]
    pick = (iota((width, column), 0) == states).astype(BF16)
    rows = dot(order_row.astype(BF16), pick, 1, 0)
    return (iota((width, column), 0) == rows.astype(jnp.int32)).astype(BF16)


def first_form(branch, order_row):
    width = order_row.shape[1]
    hot = (iota((width, width), 0) == order_row).astype(BF16)
    taken = dot(both(branch), hot, 0, 0).astype(BF16)
    real, imag = taken[:width], taken[width:]
    return jnp.concatenate(
        [jnp.concatenate([real, -imag], axis=1), jnp.concatenate([imag, real], axis=1)], axis=0
    )


def second_form(branch, order_row, part_in, me_in, part_out, me_out):
    width = order_row.shape[1]
    full = 2 * width
    comp, states = entry(iota((1, full), 1), part_in, me_in)
    hot = chosen(order_row, states, full)
    taken = dot(both(branch), hot, 0, 0)
    real, imag = taken[:width], taken[width:]
    plain = comp == 0
    form = jnp.concatenate(
        [jnp.where(plain, real, -imag), jnp.where(plain, imag, real)], axis=0
    ).astype(BF16)
    out_comp, out_states = entry(iota((full, 1), 0), part_out, me_out)
    place = (iota((full, full), 1) == out_comp * width + out_states).astype(BF16)
    return dot(place, form, 1, 0).astype(BF16)


def third_form(branch, order_row, part_in, me_in):
    width = order_row.shape[1]
    full = 2 * width
    _, states = entry(iota((1, full), 1), part_in, me_in)
    hot = chosen(order_row, states, full)
    taken = dot(hot, both(branch), 0, 0)
    real, imag = taken[:, :width], taken[:, width:]
    comp, _ = entry(iota((full, 1), 0), part_in, me_in)
    plain = comp == 0
    return jnp.concatenate(
        [jnp.where(plain, real, -imag), jnp.where(plain, imag, real)], axis=1
    ).astype(BF16)


def place_of(axis, relative):
    return lax.axis_index(axis) if relative else None


def put_first(form_ref, block, part, me, owners, outs):
    width = block.shape[2]
    form = []
    for k in owners:
        owner = k if me is None else jnp.bitwise_xor(me, k)
        form += [form_ref[pl.ds(pl.multiple_of(c * width + owner * part, part), part), :] for c in range(2)]
    joined = jnp.concatenate([block[0], block[1]], axis=1)
    result = dot(jnp.concatenate(form, axis=0), joined, 1, 1).astype(BF16)
    size = result.shape[0] // len(outs)
    for n, out in enumerate(outs):
        out[...] = result[size * n : size * (n + 1)]


def opening_kernel(part, relative, owners, stem_ref, branches_ref, order_ref, form_ref, block_ref, *rest):
    outs, (branch, order, sem) = rest[:-3], rest[-3:]
    copies = [
        pltpu.make_async_copy(order_ref, order, sem.at[0]),
        pltpu.make_async_copy(branches_ref.at[0, 0], branch.at[0], sem.at[1]),
        pltpu.make_async_copy(branches_ref.at[0, 1], branch.at[1], sem.at[3]),
        pltpu.make_async_copy(stem_ref.at[:, 0, 0, pl.ds(0, block_ref.shape[1])], block_ref, sem.at[2]),
    ]
    for copy in copies:
        copy.start()
    copies[0].wait()
    copies[1].wait()
    copies[2].wait()
    form_ref[...] = first_form(branch, order[0:1, :])
    copies[3].wait()
    put_first(form_ref, block_ref, part, place_of("mem", relative), owners, outs)


def first_kernel(part, relative, owners, n_out, block_ref, form_ref, *rest):
    put_first(form_ref, block_ref, part, place_of("mem", relative), owners, rest[-n_out:])


def forms_kernel(sizes, part1, rel1, part2, rel2, stem_ref, branches_ref, order_ref, second_ref, third_ref, *rest):
    blocks, (branch, order, sem) = rest[:-3], rest[-3:]
    copies = [
        pltpu.make_async_copy(order_ref, order, sem.at[0]),
        pltpu.make_async_copy(branches_ref.at[pl.ds(1, 2)], branch, sem.at[1]),
    ]
    lo = sizes[0]
    for n, rows in enumerate(sizes[1:]):
        copies.append(pltpu.make_async_copy(stem_ref.at[:, 0, 0, pl.ds(lo, rows)], blocks[n], sem.at[2 + n]))
        lo += rows
    for copy in copies:
        copy.start()
    copies[0].wait()
    copies[1].wait()
    me1, me2 = place_of("mem", rel1), place_of("grp", rel2)
    second_ref[...] = second_form(branch[0], order[1:2, :], part1, me1, part2, me2)
    third_ref[...] = third_form(branch[1], order[2:3, :], part2, me2)
    for copy in copies[2:]:
        copy.wait()


def gathered(refs):
    return jnp.concatenate([ref[...] for ref in refs], axis=0)


def second_kernel(n_in, slots, form_ref, *refs):
    ins, total, outs = refs[:n_in], refs[n_in : -len(slots)], refs[-len(slots) :]
    joined = gathered(ins)
    ahead = form_ref.shape[1] - joined.shape[0]
    for slot, out in zip(slots, outs):
        rows = out.shape[0]
        here = slice(rows * slot, rows * (slot + 1))
        result = dot(form_ref[here, ahead:], joined, 1, 0)
        for before in total:
            result = result + before[here]
        out[...] = result.astype(BF16)


def second_part_kernel(form_ref, *refs):
    joined = gathered(refs[:-1])
    refs[-1][...] = dot(form_ref[:, : joined.shape[0]], joined, 1, 0)


def pass_kernel(count, *refs):
    size = refs[0].shape[0] // 2
    for slot, ref in enumerate(refs[:count]):
        refs[-1][slot * size : (slot + 1) * size] = ref[size:]


def form_rows(form_ref, size, places):
    return jnp.concatenate([form_ref[size * k : size * (k + 1)] for k in places], axis=0)


def third_part_kernel(places, size, form_ref, *refs):
    joined = jnp.concatenate([ref[:size] for ref in refs[: len(places)]], axis=0)
    total = dot(joined, form_rows(form_ref, size, places), 0, 0)
    for before in refs[len(places) : -1]:
        total = total + before[...]
    refs[-1][...] = total


def block_result(places, form_ref, refs, rows):
    joined, form = refs[-1][:, rows], form_ref[...]
    if places:
        form = form_rows(form_ref, joined.shape[0] // len(places), places)
    result = dot(joined, form, 0, 0)
    return (result + refs[0][rows] if places else result).astype(BF16)


def block_kernel(places, form_ref, *refs):
    out_ref = refs[-1]
    width = out_ref.shape[2]
    result = block_result(places, form_ref, refs[:-1], slice(None))
    for c in range(2):
        out_ref[c] = result[:, c * width : (c + 1) * width]


def closing_kernel(n_done, places, form_ref, *refs):
    done, ins, (out_ref, held, sem) = refs[:n_done], refs[n_done:-3], refs[-3:]
    width, rows = held.shape[2], held.shape[1]
    copies, lo = [], 0

    def write(source, at, count):
        copies.append(pltpu.make_async_copy(source, out_ref.at[:, 0, 0, pl.ds(at, count)], sem.at[len(copies)]))
        copies[-1].start()

    for ref in done:
        write(ref, lo, ref.shape[1])
        lo += ref.shape[1]
    cut = rows // WRITE_CUT
    for at in range(0, rows, cut):
        result = block_result(places, form_ref, ins, slice(at, at + cut))
        for c in range(2):
            held[c, at : at + cut] = result[:, c * width : (c + 1) * width]
        write(held.at[:, pl.ds(at, cut)], lo + at, cut)
    for copy in copies:
        copy.wait()


ANY = pl.BlockSpec(memory_space=pl.ANY)
HBM = pl.BlockSpec(memory_space=pltpu.HBM)
VM = pl.BlockSpec(memory_space=pltpu.VMEM)


def call(kernel, in_specs, out_shapes, out_specs, cost=FREE, scratch=(), aliases={}):
    return pl.pallas_call(
        kernel,
        in_specs=in_specs,
        out_shape=out_shapes,
        out_specs=out_specs,
        scratch_shapes=list(scratch),
        input_output_aliases=aliases,
        compiler_params=pltpu.CompilerParams(vmem_limit_bytes=VMEM_LIMIT),
        cost_estimate=pl.CostEstimate(flops=cost, bytes_accessed=max(1, cost // 1000), transcendentals=0),
    )


def swap(piece, axis, count, k):
    return lax.ppermute(piece, axis, [(i, i ^ k) for i in range(count)])


def whole_exchange(whole, axis, count):
    shaped = whole.reshape(count, -1, whole.shape[-1])
    moved = lax.all_to_all(shaped, axis, split_axis=0, concat_axis=0, tiled=True)
    return moved.reshape(whole.shape)


def shape(*dims):
    return jax.ShapeDtypeStruct(dims, BF16)


def by_permutes(count):
    return 4 <= count <= PERMUTE_MAX and count & (count - 1) == 0


def local(stem, branches, mode_order):
    row_count, width = stem.shape[3], stem.shape[4]
    full = 2 * width
    inner, outer = lax.axis_size("mem"), lax.axis_size("grp")
    part1, part2 = width // inner, width // outer
    rel1, rel2 = by_permutes(inner), by_permutes(outer)
    sizes = [row_count * share // sum(ROW_SPLIT) for share in ROW_SPLIT]
    starts = [sum(sizes[:n]) for n in range(len(sizes))]
    last = len(sizes) - 1
    stem, branches, mode_order = (
        pltpu.with_memory_space_constraint(a, pltpu.HBM) for a in (stem, branches, mode_order)
    )
    form_shape = shape(full, full)
    order_scratch = pltpu.VMEM(mode_order.shape, jnp.int32)
    half = inner // 2

    def first_shapes(rows, owners):
        return [shape(full // inner, rows)] * len(owners) if rel1 else [shape(full, rows)]

    def first_pieces(block, owners, after=()):
        shapes = first_shapes(block.shape[1], owners)
        made = call(
            functools.partial(first_kernel, part1, rel1, owners, len(shapes)),
            [VM, VM] + [ANY] * len(after), shapes, [VM] * len(shapes),
        )(block, form0, *after)
        return dict(zip(owners, made))

    def inner_exchange(pieces):
        if not rel1:
            return [whole_exchange(pieces[0], "mem", inner)]
        return [pieces[0]] + [swap(pieces[k], "mem", inner, k) for k in range(1, inner)]

    everything = tuple(range(inner))
    opening = (half,) if rel1 else everything
    shapes = first_shapes(sizes[0], opening)
    form0, block, *made = call(
        functools.partial(opening_kernel, part1, rel1, opening),
        [HBM] * 3, [form_shape, shape(2, sizes[0], width)] + shapes, [VM] * (2 + len(shapes)), FREE,
        [pltpu.VMEM(branches.shape[1:], BF16), order_scratch, pltpu.SemaphoreType.DMA((4,))],
    )(stem, branches, mode_order)
    pieces = dict(zip(opening, made))
    if rel1:
        pieces.update(first_pieces(block, tuple(k for k in everything if k != half)))
    arrived = [inner_exchange(pieces)]
    form1, form2, *blocks = call(
        functools.partial(forms_kernel, sizes, part1, rel1, part2, rel2),
        [HBM] * 3, [form_shape] * 2 + [shape(2, rows, width) for rows in sizes[1:]], [VM] * (1 + len(sizes)), FREE,
        [pltpu.VMEM((2,) + branches.shape[1:], BF16), order_scratch, pltpu.SemaphoreType.DMA((1 + len(sizes),))],
    )(stem, branches, mode_order)
    for block in blocks:
        after = (form1, arrived[-1][half]) if rel1 else ()
        arrived.append(inner_exchange(first_pieces(block, everything, after)))

    pairs = outer // 2

    def second(n, slots, rows_each, cost, total=()):
        ins = arrived[n][half:] if total else arrived[n]
        shapes = [shape(rows_each, sizes[n])] * len(slots)
        made = call(
            functools.partial(second_kernel, len(ins), slots),
            [VM] * (1 + len(ins) + len(total)), shapes, [VM] * len(slots), cost,
        )(form1, *ins, *total)
        return dict(zip(slots, made))

    def third_part(n, blocks, cost, *before):
        return call(
            functools.partial(third_part_kernel, tuple(blocks), full // outer),
            [VM] * (1 + len(blocks) + len(before)), jax.ShapeDtypeStruct((sizes[n], full), F32), VM, cost,
        )(form2, *blocks.values(), *before)

    def pass_on(n, came, after=()):
        given = call(
            functools.partial(pass_kernel, len(came)),
            [VM] * len(came) + [ANY] * len(after), shape(len(came) * full // outer, sizes[n]), VM,
        )(*came.values(), *after)
        return swap(given, "grp", outer, 1), tuple(2 * q + 1 for q in came)

    def outer_exchange(n):
        slots = tuple(range(pairs))
        made = second(n, slots, full // pairs, FREE)
        came = {q: swap(made[q], "grp", outer, 2 * q) if q else made[q] for q in slots}
        total = third_part(n, {2 * q: came[q] for q in slots}, FREE)
        passed, places = pass_on(n, came, (total,))
        return [total, passed], places

    def last_exchange(n):
        slots = (0,) + tuple(range(2, pairs))
        near = ()
        if rel1:
            near = (
                call(
                    second_part_kernel, [VM] * (1 + half), jax.ShapeDtypeStruct((full, sizes[n]), F32), VM, FREE
                )(form1, *arrived[n][:half]),
            )
        made = second(n, slots[:1], full // pairs, FREE, near) | second(n, slots[1:], full // pairs, LONG, near)
        came = {q: swap(made[q], "grp", outer, 2 * q) if q else made[q] for q in slots}
        direct = second(n, (2, 3), full // outer, FREE, near)
        direct = {k: swap(direct[k], "grp", outer, k) for k in direct}
        passed, places = pass_on(n, came)
        total = third_part(n, {2 * q: came[q] for q in slots}, FREE)
        return [third_part(n, direct, LONG, total), passed], places

    done = []
    for n, rows in enumerate(sizes):
        if not rel2:
            whole = second(n, (0,), full, LONG if n == last else FREE)[0]
            ins, places = [whole_exchange(whole, "grp", outer)], ()
        else:
            ins, places = last_exchange(n) if n == last else outer_exchange(n)
        if n < last:
            kernel = functools.partial(block_kernel, places)
            done.append(call(kernel, [VM] * (1 + len(ins)), shape(2, rows, width), VM)(form2, *ins))
    return call(
        functools.partial(closing_kernel, last, places),
        [VM] * (1 + last + len(ins)), shape(*stem.shape), ANY, FREE,
        [pltpu.VMEM((2, sizes[last], width), BF16), pltpu.SemaphoreType.DMA((last + WRITE_CUT,))],
    )(form2, *done, *ins)


def solution(mesh):
    in_specs = (P(None, "grp", "mem", None, None), P(), P())
    out_specs = P(None, "grp", "mem", None, None)
    return jax.shard_map(local, mesh=mesh, in_specs=in_specs, out_specs=out_specs, check_vma=False)
```
